32 devices in a mesh: dp: 8 (over z, x), tensor: 4 (over y, core).
Axes of the slice: x: 2, y: 2, z: 4, core: 2. Of those that a mesh axis runs over, the one named last changes fastest.
Arguments:
- hidden: bfloat16 [16384, 768], P(('dp', 'tensor')), may hold values from -6 to 6
- segment_ids: int32 [16, 1024], P('dp'), may hold values from 0 to 3, as said below
- norm1_gain: float32 [768], replicated, may hold values from 0.25 to 1.75
- norm1_bias: float32 [768], replicated, may hold values from -1.75 to 1.75
- w_qkv: bfloat16 [3, 768, 768], P(None, 'dp', 'tensor'), may hold values from -0.21875 to 0.21875
- qv_bias: float32 [2, 768], P(None, 'tensor'), may hold values from -2.5 to 2.5
- w_out: bfloat16 [768, 768], P('tensor', 'dp'), may hold values from -1.75 to 1.75
- out_bias: float32 [768], replicated, may hold values from -1.75 to 1.75
- norm2_gain: float32 [768], replicated, may hold values from 0.25 to 1.75
- norm2_bias: float32 [768], replicated, may hold values from -1.75 to 1.75
- w_up: bfloat16 [768, 3072], P('dp', 'tensor'), may hold values from -0.21875 to 0.21875
- up_bias: float32 [3072], P('tensor'), may hold values from -3 to 3
- w_down: bfloat16 [3072, 768], P('tensor', 'dp'), may hold values from -0.15625 to 0.15625
- down_bias: float32 [768], replicated, may hold values from -1.75 to 1.75
- cotangent: bfloat16 [16384, 768], P(('dp', 'tensor')), may hold values from -6 to 6
Outputs:
- output: bfloat16 [16384, 768], P(('dp', 'tensor'))
- grad_hidden: bfloat16 [16384, 768], P(('dp', 'tensor'))
- grad_norm1_gain: float32 [768], replicated
- grad_norm1_bias: float32 [768], replicated
- grad_w_qkv: float32 [3, 768, 768], P(None, 'dp', 'tensor')
- grad_qv_bias: float32 [2, 768], P(None, 'tensor')
- grad_w_out: float32 [768, 768], P('tensor', 'dp')
- grad_out_bias: float32 [768], replicated
- grad_norm2_gain: float32 [768], replicated
- grad_norm2_bias: float32 [768], replicated
- grad_w_up: float32 [768, 3072], P('dp', 'tensor')
- grad_up_bias: float32 [3072], P('tensor')
- grad_w_down: float32 [3072, 768], P('tensor', 'dp')
- grad_down_bias: float32 [768], replicated
The draws below stay inside these ranges and needn't reach their ends.
Inputs may be any that keep to these rules, and one draw needn't show every extreme that they name: `segment_ids`: within a sequence the numbers never fall, and tokens of equal number form one document. In each group of 2 sequences on one index of dp, one sequence is a single document.
All inputs are finite; a program needn't handle non-finite values.
Results may differ from the reference program's by a relative error of at most 0.018.
Values may be sent and summed in bfloat16 or wider, within the bound.
No kernel may reach another device: no remote copies, remote signals or barrier semaphores. Data moves between devices by JAX's collectives and lax.ppermute only.
A program may use at most 128 MiB of HBM per device.

```python
import math
import jax
import jax.numpy as jnp
from jax import lax

D = 768
HEADS = 12
HEAD_DIM = 64
FF = 3072
SEQLEN = 1024
SEQ_DP = 2
SEQS = 16
TOKENS = 16384


def draw_segment_ids(key, part):
    key = jax.random.fold_in(key, 7)
    cut_key, whole_key = jax.random.split(key)
    spacing = SEQLEN // 8
    offsets = jax.random.randint(cut_key, (SEQS, 3), 0, SEQLEN - 4 * spacing + 1)
    cuts = jnp.sort(offsets, -1) + spacing * jnp.arange(1, 4)[None, :]
    positions = jnp.arange(SEQLEN)
    numbers = jnp.sum((positions[None, :, None] >= cuts[:, None, :]).astype(jnp.int32), -1)
    chosen = jax.random.randint(whole_key, (SEQS // SEQ_DP,), 0, SEQ_DP)
    single = jnp.arange(SEQS) % SEQ_DP == jnp.repeat(chosen, SEQ_DP)
    return jnp.where(single[:, None], 0, numbers).astype(jnp.int32)


def raised(values, own_key, source, target, parts, factor):
    owner, partner = [(jnp.arange(values.shape[axis_at]) // (values.shape[axis_at] // parts)).reshape([-1 if axis == axis_at else 1 for axis in range(values.ndim)]) for axis_at in (source, target)]
    chosen = jax.random.permutation(own_key, parts)[partner]
    strong = (owner == chosen) | (owner == (partner + parts // 2) % parts)
    return jnp.where(strong, factor * values, values)


def levels(key, dims, cuts, smallest, high):
    def one(axis_at, shards_of):
        heights = jax.random.uniform(jax.random.fold_in(jax.random.fold_in(key, 6), axis_at), (shards_of,), jnp.float32, smallest / len(cuts), high / len(cuts))
        return jnp.repeat(jnp.exp(heights), dims[axis_at] // shards_of).reshape((-1,) + (1,) * (len(dims) - axis_at - 1))

    level = one(*cuts[0])
    for cut in cuts[1:]:
        level = level * one(*cut)
    return level


def normal_values(own_key, dims, width, reach, pieces=(), kind=jnp.bfloat16):
    values = jax.random.normal(own_key, dims, jnp.float32) * width
    if len(pieces) > 0:
        values = levels(own_key, dims, pieces, -0.22, 0.18) * values
    return jnp.clip(values, min=-reach, max=reach).astype(kind)


def bell_draw_with(stream_key, dims, scale, reach, pieces, heavy, held_as=jnp.bfloat16):
    array = scale * jax.random.normal(stream_key, dims, jnp.float32)
    if pieces:
        array = array * levels(stream_key, dims, pieces, -0.22, 0.18)
    return jnp.clip(raised(array, jax.random.fold_in(stream_key, 3), *heavy), -reach, reach).astype(held_as)


def setup_inputs(seed: int = 0) -> dict:
    arg_keys = jax.random.split(jax.random.key(seed), 16)
    hidden = normal_values(arg_keys[0], (TOKENS, D), 1.0, 6.0, ((0, 32),))
    segment_ids = draw_segment_ids(jax.random.fold_in(arg_keys[15], 71), 0)
    norm1_gain = jnp.clip(1.0 + 0.15 * jax.random.normal(arg_keys[2], (D,), jnp.float32), 0.25, 1.75)
    norm1_bias = normal_values(arg_keys[3], (D,), 0.3, 1.75, (), jnp.float32)
    w_qkv = normal_values(arg_keys[4], (3, D, D), D ** -0.5, 0.21875, ((1, 8), (2, 4)))
    qv_bias = normal_values(arg_keys[5], (2, D), 0.4, 2.5, ((1, 4),), jnp.float32)
    w_out = normal_values(arg_keys[6], (D, D), (D // 64) ** -0.5, 1.75, ((0, 4), (1, 8)))
    out_bias = normal_values(arg_keys[7], (D,), 0.3, 1.75, (), jnp.float32)
    norm2_gain = jnp.clip(1.0 + 0.15 * jax.random.normal(arg_keys[8], (D,), jnp.float32), 0.25, 1.75)
    norm2_bias = normal_values(arg_keys[9], (D,), 0.3, 1.75, (), jnp.float32)
    w_up = normal_values(arg_keys[10], (D, FF), D ** -0.5, 0.21875, ((0, 8), (1, 4)))
    up_bias = normal_values(arg_keys[11], (FF,), 0.5, 3.0, ((0, 4),), jnp.float32)
    w_down = normal_values(arg_keys[12], (FF, D), (FF // 2) ** -0.5, 0.15625, ((0, 4), (1, 8)))
    down_bias = normal_values(arg_keys[13], (D,), 0.3, 1.75, (), jnp.float32)
    cotangent = bell_draw_with(arg_keys[14], (TOKENS, D), 1.0, 6.0, ((0, 32),), (0, 1, 32, 2.75))
    return dict(hidden=hidden, segment_ids=segment_ids, norm1_gain=norm1_gain, norm1_bias=norm1_bias, w_qkv=w_qkv, qv_bias=qv_bias, w_out=w_out, out_bias=out_bias, norm2_gain=norm2_gain, norm2_bias=norm2_bias, w_up=w_up, up_bias=up_bias, w_down=w_down, down_bias=down_bias, cotangent=cotangent)


@jax.custom_vjp
def low(v):
    return lax.optimization_barrier(v.astype(jnp.bfloat16)).astype(jnp.float32)

@jax.custom_vjp
def low_back(v):
    return v

def low_keep(v):
    return (low(v), None)

def low_pass(kept, grad):
    return (grad,)

def back_keep(v):
    return (v, None)

def back_low(kept, grad):
    return (low(grad),)
low.defvjp(low_keep, low_pass)
low_back.defvjp(back_keep, back_low)

def layer_norm(values, gain, bias):
    center = values - lax.optimization_barrier(jnp.mean(values, -1, keepdims=True))
    spread = lax.optimization_barrier(jnp.mean(center * center, -1, keepdims=True))
    return center * lax.rsqrt(spread + 1e-05) * gain + bias

def attend(block):
    query_group, key_group, value_group, segment_group = block
    highest = lax.Precision.HIGHEST
    scores = jnp.einsum('gqhe,gkhe->ghqk', query_group, key_group, precision=highest)
    scores = low_back(scores)
    positions = jnp.arange(SEQLEN)
    causal = positions[:, None] >= positions[None, :]
    allowed = causal[None] & (segment_group[:, :, None] == segment_group[:, None, :])
    scores = jnp.where(allowed[:, None], scores, -1e+30)
    top_score = lax.optimization_barrier(jnp.max(scores, -1, keepdims=True))
    shifted = jnp.exp(scores - top_score)
    probs = shifted / lax.optimization_barrier(jnp.sum(shifted, -1, keepdims=True))
    return jnp.einsum('ghqk,gkhe->gqhe', low(probs), value_group, precision=highest)

def forward(hidden, params, segment_ids):
    norm1_gain, norm1_bias, w_qkv, qv_bias, w_out, out_bias, norm2_gain, norm2_bias, w_up, up_bias, w_down, down_bias = params
    highest = lax.Precision.HIGHEST
    normed1 = low(layer_norm(hidden, norm1_gain, norm1_bias))
    proj = jnp.einsum('nd,cde->cne', normed1, w_qkv, precision=highest)
    queries = low(low_back((proj[0] + qv_bias[0]) * HEAD_DIM ** (-0.5)))
    keys = low(low_back(proj[1]))
    values = low(low_back(proj[2] + qv_bias[1]))
    group = math.gcd(SEQS, max(1, 4096 // SEQLEN))
    shape_five = (SEQS // group, group, SEQLEN, HEADS, HEAD_DIM)
    attended = lax.map(jax.checkpoint(attend), (queries.reshape(shape_five), keys.reshape(shape_five), values.reshape(shape_five), segment_ids.reshape(SEQS // group, group, SEQLEN)))
    attended = low(low_back(attended.reshape(TOKENS, D)))
    attn_branch = low_back(jnp.dot(attended, w_out, precision=highest, preferred_element_type=jnp.float32) + out_bias)
    mid = hidden + attn_branch
    normed2 = low(layer_norm(mid, norm2_gain, norm2_bias))
    upper = low_back(jnp.dot(normed2, w_up, precision=highest, preferred_element_type=jnp.float32) + up_bias)
    active = low(jax.nn.gelu(upper, approximate=False))
    mlp_branch = low_back(jnp.dot(active, w_down, precision=highest, preferred_element_type=jnp.float32) + down_bias)
    return mid + mlp_branch

def reference(hidden, segment_ids, norm1_gain, norm1_bias, w_qkv, qv_bias, w_out, out_bias, norm2_gain, norm2_bias, w_up, up_bias, w_down, down_bias, cotangent):
    params = (norm1_gain, norm1_bias, w_qkv.astype(jnp.float32), qv_bias, w_out.astype(jnp.float32), out_bias, norm2_gain, norm2_bias, w_up.astype(jnp.float32), up_bias, w_down.astype(jnp.float32), down_bias)
    result, pull = jax.vjp(lambda inputs, weights: forward(inputs, weights, segment_ids), hidden.astype(jnp.float32), params)
    grad_inputs, grads = pull(cotangent.astype(jnp.float32))
    return (result.astype(jnp.bfloat16), grad_inputs.astype(jnp.bfloat16), grads[0], grads[1], grads[2], grads[3], grads[4], grads[5], grads[6], grads[7], grads[8], grads[9], grads[10], grads[11])
```

```python
from functools import partial

import jax
import jax.numpy as jnp
from jax import lax
from jax.experimental import pallas as pl
from jax.experimental.pallas import tpu as pltpu
from jax.sharding import PartitionSpec as P

HEAD_DIM = 64
BLOCK = 256
LOW = jnp.bfloat16
WIDE = jnp.float32
BLOCKED = -1e30


def dot(a, b):
    return jnp.dot(a, b, preferred_element_type=WIDE)


def dot_last(a, b):
    return lax.dot_general(a, b, (((1,), (1,)), ((), ())), preferred_element_type=WIDE)


def dot_first(a, b):
    return lax.dot_general(a, b, (((0,), (0,)), ((), ())), preferred_element_type=WIDE)


def params(megabytes=40):
    return pltpu.CompilerParams(vmem_limit_bytes=megabytes * 1024 * 1024)


def cost(flops, moved, exps=0):
    return pl.CostEstimate(flops=int(flops), bytes_accessed=int(moved), transcendentals=int(exps))


def centered(values):
    center = values - jnp.mean(values, -1, keepdims=True)
    spread = jnp.mean(center * center, -1, keepdims=True)
    return center, lax.rsqrt(spread + 1e-05)


def project_kernel(x_ref, gain_ref, bias_ref, w0_ref, w1_ref, shift_ref, scale_ref, n_ref, p0_ref, p1_ref):
    center, inverse = centered(x_ref[...].astype(WIDE))
    normed = (center * inverse * gain_ref[...] + bias_ref[...]).astype(LOW)
    n_ref[...] = normed
    width = p0_ref.shape[1]
    for number, (w_ref, p_ref) in enumerate(((w0_ref, p0_ref), (w1_ref, p1_ref))):
        proj = dot(normed, w_ref[:, :width])
        p_ref[...] = ((proj + shift_ref[number : number + 1]) * scale_ref[...]).astype(LOW)


def project(both, gain, bias, w0, w1, shift, scale):
    tokens, d = both.shape[0], w0.shape[0]
    width = shift.shape[1]
    whole = lambda a: pl.BlockSpec(a.shape, lambda i: (0, 0))
    rows = lambda n: pl.BlockSpec((BLOCK, n), lambda i: (i, 0))
    return pl.pallas_call(
        project_kernel,
        grid=(tokens // BLOCK,),
        in_specs=[rows(d)] + [whole(a) for a in (gain, bias, w0, w1, shift, scale)],
        out_specs=[rows(d), rows(width), rows(width)],
        out_shape=[
            jax.ShapeDtypeStruct((tokens, d), LOW),
            jax.ShapeDtypeStruct((tokens, width), LOW),
            jax.ShapeDtypeStruct((tokens, width), LOW),
        ],
        compiler_params=params(),
        cost_estimate=cost(4 * tokens * d * width, 8 * tokens * d),
        name="project",
    )(both, gain, bias, w0, w1, shift, scale)


def features(seg, heads_values, blocked):
    lane = lax.broadcasted_iota(jnp.int32, (seg.shape[0], HEAD_DIM), 1)
    same = lane == seg
    if blocked:
        extra = jnp.where(same | (lane > 3), 0.0, BLOCKED)
    else:
        extra = jnp.where(same, 1.0, 0.0)
    return jnp.concatenate([heads_values, extra.astype(LOW)], axis=1)


def causal(scores_t):
    key = lax.broadcasted_iota(jnp.int32, scores_t.shape, 0)
    query = lax.broadcasted_iota(jnp.int32, scores_t.shape, 1)
    return jnp.where(key <= query, scores_t, BLOCKED)


def attend_kernel(p_ref, seg_ref, out_ref, log_ref):
    length = p_ref.shape[0]
    heads = p_ref.shape[1] // (3 * HEAD_DIM)
    seg = seg_ref[...]
    logs = []
    outs = [jnp.zeros((length, HEAD_DIM), LOW)]
    for head in range(heads):
        at = lambda c: slice((c * heads + head) * HEAD_DIM, (c * heads + head + 1) * HEAD_DIM)
        query = features(seg, p_ref[:, at(0)], True)
        key = features(seg, p_ref[:, at(1)], False)
        value = p_ref[:, at(2)]
        head_logs, head_outs = [], []
        for block in range(length // BLOCK):
            start, stop = block * BLOCK, (block + 1) * BLOCK
            scores = dot_last(key[:stop], query[start:stop])
            last = causal(scores[start:])
            scores = last if block == 0 else jnp.concatenate([scores[:start], last], axis=0)
            top = jnp.max(scores, 0, keepdims=True)
            shifted = jnp.exp(scores - top)
            total = jnp.sum(shifted, 0, keepdims=True)
            result = dot_first(value[:stop], shifted.astype(LOW)) / total
            head_logs.append(top + jnp.log(total))
            head_outs.append(result.T.astype(LOW))
        logs.append(jnp.concatenate(head_logs, axis=1))
        outs.append(jnp.concatenate(head_outs, axis=0))
    out_ref[...] = jnp.concatenate(outs, axis=1)
    logs.append(jnp.zeros((8 - heads, length), WIDE))
    log_ref[...] = jnp.concatenate(logs, axis=0)


def attend(proj, seg):
    length, width = proj.shape
    heads = width // (3 * HEAD_DIM)
    return pl.pallas_call(
        attend_kernel,
        out_shape=[
            jax.ShapeDtypeStruct((length, (heads + 1) * HEAD_DIM), LOW),
            jax.ShapeDtypeStruct((8, length), WIDE),
        ],
        compiler_params=params(),
        cost_estimate=cost(heads * 4 * length * length * HEAD_DIM, 4 * length * width, heads * length * length),
        name="attend",
    )(proj, seg)


def attend_back_kernel(p_ref, seg_ref, out_ref, log_ref, grad_ref, gp_ref, sum_ref, dq_ref):
    length = p_ref.shape[0]
    heads = p_ref.shape[1] // (3 * HEAD_DIM)
    seg = seg_ref[...]
    pieces = [[], [], []]
    for head in range(heads):
        at = lambda c: slice((c * heads + head) * HEAD_DIM, (c * heads + head + 1) * HEAD_DIM)
        shifted_at = slice((head + 1) * HEAD_DIM, (head + 2) * HEAD_DIM)
        plain = p_ref[:, at(0)]
        query = features(seg, plain, True)
        plain_key = p_ref[:, at(1)]
        key = features(seg, plain_key, False)
        value = p_ref[:, at(2)]
        grad = grad_ref[:, shifted_at]
        log_row = log_ref[head : head + 1]
        product = grad.astype(WIDE) * out_ref[:, shifted_at].astype(WIDE)
        inner = jnp.sum(product.T, 0, keepdims=True)
        dks, dvs = [], []
        for block in range(length // BLOCK):
            start, stop = block * BLOCK, (block + 1) * BLOCK
            scores = dot_last(key[start:stop], query[start:])
            first = causal(scores[:, :BLOCK])
            if stop < length:
                first = jnp.concatenate([first, scores[:, BLOCK:]], axis=1)
            probs = jnp.exp(first - log_row[:, start:])
            grad_probs = dot_last(value[start:stop], grad[start:])
            grad_scores = (probs * (grad_probs - inner[:, start:])).astype(LOW)
            dvs.append(dot(probs.astype(LOW), grad[start:]).astype(LOW))
            dks.append(dot(grad_scores, plain[start:]).astype(LOW))
            part = dot_first(plain_key[start:stop], grad_scores)
            if block == 0:
                dq_ref[...] = part
            else:
                dq_ref[:, start:] += part
        dq = (dq_ref[...].T.astype(LOW).astype(WIDE) * HEAD_DIM ** (-0.5)).astype(LOW)
        pieces[0].append(dq)
        pieces[1].append(jnp.concatenate(dks, axis=0))
        pieces[2].append(jnp.concatenate(dvs, axis=0))
    grads = jnp.concatenate(pieces[0] + pieces[1] + pieces[2], axis=1)
    gp_ref[...] = grads
    sum_ref[...] = jnp.sum(grads.astype(WIDE), 0, keepdims=True)


def attend_back(proj, seg, out, logs, grad):
    length, width = proj.shape
    heads = width // (3 * HEAD_DIM)
    return pl.pallas_call(
        attend_back_kernel,
        out_shape=[
            jax.ShapeDtypeStruct((length, width), LOW),
            jax.ShapeDtypeStruct((1, width), WIDE),
        ],
        scratch_shapes=[pltpu.VMEM((HEAD_DIM, length), WIDE)],
        compiler_params=params(),
        cost_estimate=cost(heads * 10 * length * length * HEAD_DIM, 8 * length * width, heads * length * length),
        name="attend_back",
    )(proj, seg, out, logs, grad)


def mlp_kernel(
    x_ref, cot_ref, pa_ref, pb_ref, ob_ref, gain_ref, bias_ref, ub_ref, up0_ref, up1_ref, dn0_ref, dn1_ref,
    mid_ref, n_ref, act_ref, gu_ref, mlp_ref, gn_ref, sum_ref,
):
    middle = x_ref[...].astype(WIDE) + (pa_ref[...].astype(WIDE) + pb_ref[...].astype(WIDE)) + ob_ref[...]
    mid_ref[...] = middle
    center, inverse = centered(middle)
    normed = (center * inverse * gain_ref[...] + bias_ref[...]).astype(LOW)
    n_ref[...] = normed
    cot = cot_ref[...]
    width = up0_ref.shape[1]
    chunk = width // 2

    @pl.when(pl.program_id(0) == 0)
    def _():
        sum_ref[...] = jnp.zeros_like(sum_ref)

    mlp = grad_normed = None
    for number, (up_ref, dn_ref) in enumerate(((up0_ref, dn0_ref), (up1_ref, dn1_ref))):
        for start in range(0, width, chunk):
            at = slice(start, start + chunk)
            to = slice(number * width + start, number * width + start + chunk)
            upper = dot(normed, up_ref[:, at]) + ub_ref[number : number + 1, at]
            grad_active = dot(cot, dn_ref[:, at])
            phi = 0.5 + 0.5 * lax.erf(upper * 0.5**0.5)
            density = jnp.exp(-0.5 * (upper * upper)) * 0.3989422804014327
            active = (upper * phi).astype(LOW)
            grad_upper = (grad_active * (phi + upper * density)).astype(LOW)
            act_ref[:, to] = active
            gu_ref[:, to] = grad_upper
            sum_ref[:, to] += jnp.sum(grad_upper.astype(WIDE), 0, keepdims=True)
            a = dot_last(active, dn_ref[:, at])
            b = dot_last(grad_upper, up_ref[:, at])
            mlp = a if mlp is None else mlp + a
            grad_normed = b if grad_normed is None else grad_normed + b
    mlp_ref[...] = mlp.astype(LOW)
    gn_ref[...] = grad_normed.astype(LOW)


def mlp_pass(both, pa, pb, out_bias, gain, bias, up_bias, up0, up1, dn0, dn1):
    tokens, d = pa.shape
    width = up0.shape[1]
    whole = lambda a: pl.BlockSpec(a.shape, lambda i: (0, 0))
    rows = lambda n: pl.BlockSpec((BLOCK, n), lambda i: (i, 0))
    shape = jax.ShapeDtypeStruct
    return pl.pallas_call(
        mlp_kernel,
        grid=(tokens // BLOCK,),
        in_specs=[rows(d), pl.BlockSpec((BLOCK, d), lambda i: (i, 1)), rows(d), rows(d)]
        + [whole(a) for a in (out_bias, gain, bias, up_bias, up0, up1, dn0, dn1)],
        out_specs=[rows(d), rows(d), rows(2 * width), rows(2 * width), rows(d), rows(d)]
        + [pl.BlockSpec((1, 2 * width), lambda i: (0, 0))],
        out_shape=[
            shape((tokens, d), WIDE),
            shape((tokens, d), LOW),
            shape((tokens, 2 * width), LOW),
            shape((tokens, 2 * width), LOW),
            shape((tokens, d), LOW),
            shape((tokens, d), LOW),
            shape((1, 2 * width), WIDE),
        ],
        compiler_params=params(),
        cost_estimate=cost(16 * tokens * d * width, 30 * tokens * d, 4 * tokens * width),
        name="mlp_pass",
    )(both, both, pa, pb, out_bias, gain, bias, up_bias, up0, up1, dn0, dn1)


def norm_back_kernel(mid_ref, cot_ref, ga_ref, gb_ref, gain_ref, w0_ref, w1_ref, gm_ref, low_ref, g0_ref, g1_ref, sum_ref):
    e = ga_ref[...].astype(WIDE) + gb_ref[...].astype(WIDE)
    cot = cot_ref[...].astype(WIDE)
    center, inverse = centered(mid_ref[...])
    normal = center * inverse
    f = e * gain_ref[...]
    grad = inverse * (f - jnp.mean(f, -1, keepdims=True) - normal * jnp.mean(f * normal, -1, keepdims=True))
    grad_mid = cot + grad
    gm_ref[...] = grad_mid
    low = grad_mid.astype(LOW)
    low_ref[...] = low
    split = w0_ref.shape[1] - g0_ref.shape[1]
    g0_ref[...] = dot(low, w0_ref[:, split:]).astype(LOW)
    g1_ref[...] = dot(low, w1_ref[:, split:]).astype(LOW)

    @pl.when(pl.program_id(0) == 0)
    def _():
        sum_ref[...] = jnp.zeros_like(sum_ref)

    for row, term in enumerate((e * normal, e, low.astype(WIDE), cot)):
        sum_ref[row : row + 1] += jnp.sum(term, 0, keepdims=True)


def norm_back(mid, both, ga, gb, gain, w0, w1, width):
    tokens, d = mid.shape
    whole = lambda a: pl.BlockSpec(a.shape, lambda i: (0, 0))
    rows = lambda n: pl.BlockSpec((BLOCK, n), lambda i: (i, 0))
    shape = jax.ShapeDtypeStruct
    return pl.pallas_call(
        norm_back_kernel,
        grid=(tokens // BLOCK,),
        in_specs=[rows(d), pl.BlockSpec((BLOCK, d), lambda i: (i, 1)), rows(d), rows(d)]
        + [whole(a) for a in (gain, w0, w1)],
        out_specs=[rows(d), rows(d), rows(width), rows(width), pl.BlockSpec((8, d), lambda i: (0, 0))],
        out_shape=[
            shape((tokens, d), WIDE),
            shape((tokens, d), LOW),
            shape((tokens, width), LOW),
            shape((tokens, width), LOW),
            shape((8, d), WIDE),
        ],
        compiler_params=params(),
        cost_estimate=cost(4 * tokens * d * width, 20 * tokens * d),
        name="norm_back",
    )(mid, both, ga, gb, gain, w0, w1)


def swap(value, axis, bit):
    size = lax.axis_size(axis)
    return lax.ppermute(value, axis, [(i, i ^ bit) for i in range(size)])


def has(axis, bit):
    return (lax.axis_index(axis) // bit) % 2 == 1


def in_order(flag, own, other, axis):
    return jnp.concatenate([jnp.where(flag, other, own), jnp.where(flag, own, other)], axis=axis)


def far_bits(size):
    bit, bits = size // 2, []
    while bit > 1:
        bits.append(bit)
        bit //= 2
    return bits


def spread_far(piece):
    held = piece[None]
    for level, bit in enumerate(far_bits(lax.axis_size("dp"))):
        held = in_order(has("dp", bit), held[:, None], swap(held, "dp", bit)[:, None], 1)
        held = held.reshape((2 ** (level + 1),) + piece.shape)
    return held


def rows_of(parts, mine):
    ordered = in_order(has("dp", 1), parts[:, None], mine[:, None], 1)
    return ordered.reshape(-1, parts.shape[-1])


def spread_x_first(held):
    own = rows_of(held, swap(held, "dp", 1))
    return own, swap(own, "tensor", 2)


def spread_y_first(held):
    pair = jnp.stack([held, swap(held, "tensor", 2)])
    there = swap(pair, "dp", 1)
    return rows_of(pair[0], there[0]), rows_of(pair[1], there[1])


def halves(grad):
    size = lax.axis_size("dp")
    parts = grad.reshape(size // 2, 2, grad.shape[0] // size, grad.shape[1])
    flag = has("dp", 1)
    return jnp.where(flag, parts[:, 1], parts[:, 0]), jnp.where(flag, parts[:, 0], parts[:, 1])


def added(a, b):
    return (a.astype(WIDE) + b.astype(WIDE)).astype(LOW)


def collect_y_first(own, other):
    kept, sent = halves(added(own, swap(other, "tensor", 2)))
    return added(kept, swap(sent, "dp", 1))


def collect_x_first(own, other):
    kept_own, sent_own = halves(own)
    kept_other, sent_other = halves(other)
    there = swap(jnp.stack([sent_own, sent_other]), "dp", 1)
    return added(added(kept_own, there[0]), swap(added(kept_other, there[1]), "tensor", 2))


def collect_far(held):
    for bit in reversed(far_bits(lax.axis_size("dp"))):
        pairs = held.reshape((held.shape[0] // 2, 2) + held.shape[1:])
        flag = has("dp", bit)
        kept = jnp.where(flag, pairs[:, 1], pairs[:, 0])
        sent = jnp.where(flag, pairs[:, 0], pairs[:, 1])
        held = kept.astype(WIDE) + swap(sent, "dp", bit).astype(WIDE)
        if held.shape[0] > 1:
            held = held.astype(LOW)
    return held[0].astype(WIDE)


def body(
    hidden, segment_ids, norm1_gain, norm1_bias, w_qkv, qv_bias, w_out, out_bias,
    norm2_gain, norm2_bias, w_up, up_bias, w_down, down_bias, cotangent,
):
    mine, d = hidden.shape
    shard, width = w_qkv.shape[1], w_qkv.shape[2]
    core = has("tensor", 1)
    row = lambda v: v.reshape(1, -1)

    first = jnp.concatenate([w_qkv[0], w_qkv[1], w_qkv[2], w_out.T], axis=1)
    second = jnp.concatenate([w_up, w_down.T], axis=1)
    far_first = spread_far(first)
    a0, a1 = spread_x_first(far_first[..., : 2 * width])
    b0, b1 = spread_y_first(far_first[..., 2 * width :])
    w0, w1 = jnp.concatenate([a0, b0], axis=1), jnp.concatenate([a1, b1], axis=1)
    far_second = spread_far(second)
    up0, up1 = spread_x_first(far_second[..., : w_up.shape[1]])
    dn0, dn1 = spread_y_first(far_second[..., w_up.shape[1] :])
    biases = jnp.concatenate([qv_bias.reshape(-1), up_bias])
    other_biases = swap(biases, "tensor", 2)
    ub = jnp.stack([up_bias, other_biases[2 * width :]])
    none = jnp.zeros((width,), WIDE)
    shift = jnp.stack(
        [jnp.concatenate([v[:width], none, v[width : 2 * width]]) for v in (biases, other_biases)]
    )
    scale = jnp.concatenate([none + HEAD_DIM ** (-0.5), none + 1.0, none + 1.0]).reshape(1, -1)

    pair = jnp.concatenate([hidden, cotangent], axis=1)
    both = in_order(core, pair, swap(pair, "tensor", 1), 0)
    seg = lax.dynamic_index_in_dim(segment_ids, lax.axis_index("tensor") // 2, 0, keepdims=False)
    seg = seg.reshape(-1, 1)
    here = lax.axis_index("tensor") % 2 * mine
    there = mine - here

    n1, p0, p1 = project(both, row(norm1_gain), row(norm1_bias), w0, w1, shift, scale)
    att0, log0 = attend(p0, seg)
    att1, log1 = attend(p1, seg)
    cut = w0.shape[1] - att0.shape[1]
    pa = (dot_last(att0, w0[:, cut:]) + dot_last(att1, w1[:, cut:])).astype(LOW)
    pb = swap(pa, "tensor", 1)
    middle, n2, active, grad_upper, mlp, ga, up_sums = mlp_pass(
        both, pa, pb, row(out_bias), row(norm2_gain), row(norm2_bias), ub, up0, up1, dn0, dn1
    )
    mlp_there = swap(lax.dynamic_slice_in_dim(mlp, there, mine, 0), "tensor", 1)
    mlp_here = lax.dynamic_slice_in_dim(mlp, here, mine, 0)
    output = lax.dynamic_slice_in_dim(middle, here, mine, 0) + down_bias
    output = (output + (mlp_here.astype(WIDE) + mlp_there.astype(WIDE))).astype(LOW)

    gb = swap(ga, "tensor", 1)
    cot_all = both[:, d:]
    half = w_up.shape[1]
    low_dot = lambda a, b: dot_first(a, b).astype(LOW)
    grad_mid, grad_attn, gatt0, gatt1, sums = norm_back(
        middle, both, ga, gb, row(norm2_gain), w0, w1, att0.shape[1]
    )
    down = collect_y_first(low_dot(cot_all, active[:, :half]), low_dot(cot_all, active[:, half:]))
    up = collect_x_first(low_dot(n2, grad_upper[:, :half]), low_dot(n2, grad_upper[:, half:]))
    second_grad = collect_far(jnp.concatenate([up, down], axis=2))

    gp0, gsum0 = attend_back(p0, seg, att0, log0, gatt0)
    gp1, gsum1 = attend_back(p1, seg, att1, log1, gatt1)

    def branch(start):
        cut_rows = lambda v: lax.dynamic_slice_in_dim(v, start, mine, 0)
        return dot_last(cut_rows(gp0), w0[:, : 3 * width]) + dot_last(cut_rows(gp1), w1[:, : 3 * width])

    from_there = swap(branch(there).astype(LOW), "tensor", 1)
    grad_normed1 = branch(here) + from_there.astype(WIDE)

    tail0, tail1 = [
        jnp.concatenate([low_dot(n1, gp[:, 2 * width :]), low_dot(grad_attn, att[:, HEAD_DIM:])], axis=1)
        for gp, att in ((gp0, att0), (gp1, att1))
    ]
    front = collect_x_first(low_dot(n1, gp0[:, : 2 * width]), low_dot(n1, gp1[:, : 2 * width]))
    tail = collect_y_first(tail0, tail1)
    first_grad = collect_far(jnp.concatenate([front, tail], axis=2))

    center, inverse = centered(hidden.astype(WIDE))
    normal = center * inverse
    f = grad_normed1 * norm1_gain
    grad_input = inverse * (f - jnp.mean(f, -1, keepdims=True) - normal * jnp.mean(f * normal, -1, keepdims=True))
    grad_hidden = (lax.dynamic_slice_in_dim(grad_mid, here, mine, 0) + grad_input).astype(LOW)

    norm1_sums = jnp.stack([jnp.sum(grad_normed1 * normal, 0), jnp.sum(grad_normed1, 0)])
    norm1_sums = norm1_sums + swap(norm1_sums, "tensor", 1)
    shared = jnp.concatenate([norm1_sums.reshape(-1), sums[:4].reshape(-1)])
    part = lambda gsum, at: jnp.concatenate(
        [gsum[0, :width], gsum[0, 2 * width :], up_sums[0, at : at + half]]
    )
    sent = swap(jnp.concatenate([shared, part(gsum1, half)]), "tensor", 2)
    total = jnp.concatenate([shared, part(gsum0, 0)]) + sent
    bit = 1
    while bit < lax.axis_size("dp"):
        total = total + swap(total, "dp", bit)
        bit *= 2
    norm1_gain_grad, norm1_bias_grad, gain2, bias2, out_grad, down_grad = (
        total[i * d : (i + 1) * d] for i in range(6)
    )
    own = total[6 * d :]
    columns = lambda i: first_grad[:, i * width : (i + 1) * width]
    return (
        output,
        grad_hidden,
        norm1_gain_grad,
        norm1_bias_grad,
        jnp.stack([columns(0), columns(1), columns(2)]),
        own[: 2 * width].reshape(2, width),
        columns(3).T,
        out_grad,
        gain2,
        bias2,
        second_grad[:, :half],
        own[2 * width :],
        second_grad[:, half:].T,
        down_grad,
    )


def solution(mesh):
    placed = (
        P(("dp", "tensor"), None),
        P("dp", None),
        P(),
        P(),
        P(None, "dp", "tensor"),
        P(None, "tensor"),
        P("tensor", "dp"),
        P(),
        P(),
        P(),
        P("dp", "tensor"),
        P("tensor"),
        P("tensor", "dp"),
        P(),
        P(("dp", "tensor"), None),
    )
    return jax.shard_map(
        body,
        mesh=mesh,
        in_specs=placed,
        out_specs=(
            P(("dp", "tensor"), None),
            P(("dp", "tensor"), None),
            P(),
            P(),
            P(None, "dp", "tensor"),
            P(None, "tensor"),
            P("tensor", "dp"),
            P(),
            P(),
            P(),
            P("dp", "tensor"),
            P("tensor"),
            P("tensor", "dp"),
            P(),
        ),
        check_vma=False,
    )
```

```python
from functools import partial

import jax
import jax.numpy as jnp
from jax import lax
from jax.experimental import pallas as pl
from jax.experimental.pallas import tpu as pltpu
from jax.sharding import PartitionSpec as P

HEAD_DIM = 64
BLOCK = 256
LOW = jnp.bfloat16
WIDE = jnp.float32
BLOCKED = -1e30


def dot(a, b):
    return jnp.dot(a, b, preferred_element_type=WIDE)


def dot_last(a, b):
    return lax.dot_general(a, b, (((1,), (1,)), ((), ())), preferred_element_type=WIDE)


def dot_first(a, b):
    return lax.dot_general(a, b, (((0,), (0,)), ((), ())), preferred_element_type=WIDE)


def params(megabytes=40):
    return pltpu.CompilerParams(vmem_limit_bytes=megabytes * 1024 * 1024)


def cost(micros):
    return pl.CostEstimate(flops=int(micros * 1.15e9), bytes_accessed=0, transcendentals=0)


def centered(values):
    center = values - jnp.mean(values, -1, keepdims=True)
    spread = jnp.mean(center * center, -1, keepdims=True)
    return center, lax.rsqrt(spread + 1e-05)


def project_kernel(x_ref, gain_ref, bias_ref, w0_ref, w1_ref, shift_ref, scale_ref, n_ref, p0_ref, p1_ref):
    center, inverse = centered(x_ref[...].astype(WIDE))
    normed = (center * inverse * gain_ref[...] + bias_ref[...]).astype(LOW)
    n_ref[...] = normed
    width = p0_ref.shape[1]
    for number, (w_ref, p_ref) in enumerate(((w0_ref, p0_ref), (w1_ref, p1_ref))):
        proj = dot(normed, w_ref[:, :width])
        p_ref[...] = ((proj + shift_ref[number : number + 1]) * scale_ref[...]).astype(LOW)


def project(both, gain, bias, w0, w1, shift, scale):
    tokens, d = both.shape[0], w0.shape[0]
    width = shift.shape[1]
    whole = lambda a: pl.BlockSpec(a.shape, lambda i: (0, 0))
    rows = lambda n: pl.BlockSpec((BLOCK, n), lambda i: (i, 0))
    return pl.pallas_call(
        project_kernel,
        grid=(tokens // BLOCK,),
        in_specs=[rows(d)] + [whole(a) for a in (gain, bias, w0, w1, shift, scale)],
        out_specs=[rows(d), rows(width), rows(width)],
        out_shape=[
            jax.ShapeDtypeStruct((tokens, d), LOW),
            jax.ShapeDtypeStruct((tokens, width), LOW),
            jax.ShapeDtypeStruct((tokens, width), LOW),
        ],
        compiler_params=params(),
        cost_estimate=cost(4.6),
        name="project",
    )(both, gain, bias, w0, w1, shift, scale)


def features(seg, heads_values, blocked):
    lane = lax.broadcasted_iota(jnp.int32, (seg.shape[0], HEAD_DIM), 1)
    same = lane == seg
    if blocked:
        extra = jnp.where(same | (lane > 3), 0.0, BLOCKED)
    else:
        extra = jnp.where(same, 1.0, 0.0)
    return jnp.concatenate([heads_values, extra.astype(LOW)], axis=1)


def causal(scores_t):
    key = lax.broadcasted_iota(jnp.int32, scores_t.shape, 0)
    query = lax.broadcasted_iota(jnp.int32, scores_t.shape, 1)
    return jnp.where(key <= query, scores_t, BLOCKED)


def attend_kernel(p_ref, seg_ref, out_ref, log_ref):
    length = p_ref.shape[0]
    heads = p_ref.shape[1] // (3 * HEAD_DIM)
    seg = seg_ref[...]
    logs = []
    outs = [jnp.zeros((length, HEAD_DIM), LOW)]
    for head in range(heads):
        at = lambda c: slice((c * heads + head) * HEAD_DIM, (c * heads + head + 1) * HEAD_DIM)
        query = features(seg, p_ref[:, at(0)], True)
        key = features(seg, p_ref[:, at(1)], False)
        value = p_ref[:, at(2)]
        head_logs, head_outs = [], []
        for block in range(length // BLOCK):
            start, stop = block * BLOCK, (block + 1) * BLOCK
            scores = dot_last(key[:stop], query[start:stop])
            last = causal(scores[start:])
            scores = last if block == 0 else jnp.concatenate([scores[:start], last], axis=0)
            top = jnp.max(scores, 0, keepdims=True)
            shifted = jnp.exp(scores - top)
            total = jnp.sum(shifted, 0, keepdims=True)
            result = dot_first(value[:stop], shifted.astype(LOW)) / total
            head_logs.append(top + jnp.log(total))
            head_outs.append(result.T.astype(LOW))
        logs.append(jnp.concatenate(head_logs, axis=1))
        outs.append(jnp.concatenate(head_outs, axis=0))
    out_ref[...] = jnp.concatenate(outs, axis=1)
    logs.append(jnp.zeros((8 - heads, length), WIDE))
    log_ref[...] = jnp.concatenate(logs, axis=0)


def attend(proj, seg):
    length, width = proj.shape
    heads = width // (3 * HEAD_DIM)
    return pl.pallas_call(
        attend_kernel,
        out_shape=[
            jax.ShapeDtypeStruct((length, (heads + 1) * HEAD_DIM), LOW),
            jax.ShapeDtypeStruct((8, length), WIDE),
        ],
        compiler_params=params(),
        cost_estimate=cost(5.4),
        name="attend",
    )(proj, seg)


def attend_back_kernel(p_ref, seg_ref, out_ref, log_ref, grad_ref, gp_ref, sum_ref, dq_ref):
    length = p_ref.shape[0]
    heads = p_ref.shape[1] // (3 * HEAD_DIM)
    seg = seg_ref[...]
    pieces = [[], [], []]
    for head in range(heads):
        at = lambda c: slice((c * heads + head) * HEAD_DIM, (c * heads + head + 1) * HEAD_DIM)
        shifted_at = slice((head + 1) * HEAD_DIM, (head + 2) * HEAD_DIM)
        plain = p_ref[:, at(0)]
        query = features(seg, plain, True)
        plain_key = p_ref[:, at(1)]
        key = features(seg, plain_key, False)
        value = p_ref[:, at(2)]
        grad = grad_ref[:, shifted_at]
        log_row = log_ref[head : head + 1]
        product = grad.astype(WIDE) * out_ref[:, shifted_at].astype(WIDE)
        inner = jnp.sum(product.T, 0, keepdims=True)
        dks, dvs = [], []
        for block in range(length // BLOCK):
            start, stop = block * BLOCK, (block + 1) * BLOCK
            scores = dot_last(key[start:stop], query[start:])
            first = causal(scores[:, :BLOCK])
            if stop < length:
                first = jnp.concatenate([first, scores[:, BLOCK:]], axis=1)
            probs = jnp.exp(first - log_row[:, start:])
            grad_probs = dot_last(value[start:stop], grad[start:])
            grad_scores = (probs * (grad_probs - inner[:, start:])).astype(LOW)
            dvs.append(dot(probs.astype(LOW), grad[start:]).astype(LOW))
            dks.append(dot(grad_scores, plain[start:]).astype(LOW))
            part = dot_first(plain_key[start:stop], grad_scores)
            if block == 0:
                dq_ref[...] = part
            else:
                dq_ref[:, start:] += part
        dq = (dq_ref[...].T.astype(LOW).astype(WIDE) * HEAD_DIM ** (-0.5)).astype(LOW)
        pieces[0].append(dq)
        pieces[1].append(jnp.concatenate(dks, axis=0))
        pieces[2].append(jnp.concatenate(dvs, axis=0))
    grads = jnp.concatenate(pieces[0] + pieces[1] + pieces[2], axis=1)
    gp_ref[...] = grads
    sum_ref[...] = jnp.sum(grads.astype(WIDE), 0, keepdims=True)


def attend_back(proj, seg, out, logs, grad):
    length, width = proj.shape
    heads = width // (3 * HEAD_DIM)
    return pl.pallas_call(
        attend_back_kernel,
        out_shape=[
            jax.ShapeDtypeStruct((length, width), LOW),
            jax.ShapeDtypeStruct((1, width), WIDE),
        ],
        scratch_shapes=[pltpu.VMEM((HEAD_DIM, length), WIDE)],
        compiler_params=params(),
        cost_estimate=cost(5.7),
        name="attend_back",
    )(proj, seg, out, logs, grad)


def mlp_kernel(opening, *refs):
    if opening:
        x_ref, cot_ref, pa_ref, pb_ref, ob_ref, gain_ref, bias_ref, ub_ref, up_ref, dn_ref = refs[:10]
        act_ref, gu_ref, mlp_ref, gn_ref, sum_ref, mid_ref, n_ref = refs[10:]
        middle = x_ref[...].astype(WIDE) + (pa_ref[...].astype(WIDE) + pb_ref[...].astype(WIDE)) + ob_ref[...]
        mid_ref[...] = middle
        center, inverse = centered(middle)
        normed = (center * inverse * gain_ref[...] + bias_ref[...]).astype(LOW)
        n_ref[...] = normed
        mlp = grad_normed = None
    else:
        n_ref, cot_ref, before_ref, grad_before_ref, ub_ref, up_ref, dn_ref = refs[:7]
        act_ref, gu_ref, mlp_ref, gn_ref, sum_ref = refs[7:]
        normed = n_ref[...]
        mlp, grad_normed = before_ref[...], grad_before_ref[...]
    cot = cot_ref[...]
    width = up_ref.shape[1]
    chunk = 256

    @pl.when(pl.program_id(0) == 0)
    def _():
        sum_ref[...] = jnp.zeros_like(sum_ref)

    for start in range(0, width, chunk):
        at = slice(start, start + chunk)
        upper = dot(normed, up_ref[:, at]) + ub_ref[:, at]
        grad_active = dot(cot, dn_ref[:, at])
        phi = 0.5 + 0.5 * lax.erf(upper * 0.5**0.5)
        density = jnp.exp(-0.5 * (upper * upper)) * 0.3989422804014327
        active = (upper * phi).astype(LOW)
        grad_upper = (grad_active * (phi + upper * density)).astype(LOW)
        act_ref[:, at] = active
        gu_ref[:, at] = grad_upper
        sum_ref[:, at] += jnp.sum(grad_upper.astype(WIDE), 0, keepdims=True)
        a = dot_last(active, dn_ref[:, at])
        b = dot_last(grad_upper, up_ref[:, at])
        mlp = a if mlp is None else mlp + a
        grad_normed = b if grad_normed is None else grad_normed + b
    mlp_ref[...] = mlp.astype(mlp_ref.dtype)
    gn_ref[...] = grad_normed.astype(gn_ref.dtype)


def mlp_pass(opening, lead, both, others, up_bias, up, dn):
    tokens, d = both.shape[0], up.shape[0]
    width = up.shape[1]
    whole = lambda a: pl.BlockSpec(a.shape, lambda i: (0, 0))
    rows = lambda n: pl.BlockSpec((BLOCK, n), lambda i: (i, 0))
    shape = jax.ShapeDtypeStruct
    spec_of = lambda a: rows(a.shape[1]) if a.shape[0] == tokens else whole(a)
    kind = WIDE if opening else LOW
    out_specs = [rows(width), rows(width), rows(d), rows(d), pl.BlockSpec((1, width), lambda i: (0, 0))]
    out_shape = [
        shape((tokens, width), LOW),
        shape((tokens, width), LOW),
        shape((tokens, d), kind),
        shape((tokens, d), kind),
        shape((1, width), WIDE),
    ]
    if opening:
        out_specs += [rows(d), rows(d)]
        out_shape += [shape((tokens, d), WIDE), shape((tokens, d), LOW)]
    return pl.pallas_call(
        partial(mlp_kernel, opening),
        grid=(tokens // BLOCK,),
        in_specs=[rows(d), pl.BlockSpec((BLOCK, d), lambda i: (i, 1))]
        + [spec_of(a) for a in others]
        + [whole(a) for a in (up_bias, up, dn)],
        out_specs=out_specs,
        out_shape=out_shape,
        compiler_params=params(),
        cost_estimate=cost(10),
        name="mlp_first" if opening else "mlp_second",
    )(lead, both, *others, up_bias, up, dn)


def norm_back_kernel(mid_ref, cot_ref, ga_ref, gb_ref, gain_ref, w0_ref, w1_ref, gm_ref, low_ref, g0_ref, g1_ref, sum_ref):
    e = ga_ref[...].astype(WIDE) + gb_ref[...].astype(WIDE)
    cot = cot_ref[...].astype(WIDE)
    center, inverse = centered(mid_ref[...])
    normal = center * inverse
    f = e * gain_ref[...]
    grad = inverse * (f - jnp.mean(f, -1, keepdims=True) - normal * jnp.mean(f * normal, -1, keepdims=True))
    grad_mid = cot + grad
    gm_ref[...] = grad_mid
    low = grad_mid.astype(LOW)
    low_ref[...] = low
    split = w0_ref.shape[1] - g0_ref.shape[1]
    g0_ref[...] = dot(low, w0_ref[:, split:]).astype(LOW)
    g1_ref[...] = dot(low, w1_ref[:, split:]).astype(LOW)

    @pl.when(pl.program_id(0) == 0)
    def _():
        sum_ref[...] = jnp.zeros_like(sum_ref)

    for row, term in enumerate((e * normal, e, low.astype(WIDE), cot)):
        sum_ref[row : row + 1] += jnp.sum(term, 0, keepdims=True)


def norm_back(mid, both, ga, gb, gain, w0, w1, width):
    tokens, d = mid.shape
    whole = lambda a: pl.BlockSpec(a.shape, lambda i: (0, 0))
    rows = lambda n: pl.BlockSpec((BLOCK, n), lambda i: (i, 0))
    shape = jax.ShapeDtypeStruct
    return pl.pallas_call(
        norm_back_kernel,
        grid=(tokens // BLOCK,),
        in_specs=[rows(d), pl.BlockSpec((BLOCK, d), lambda i: (i, 1)), rows(d), rows(d)]
        + [whole(a) for a in (gain, w0, w1)],
        out_specs=[rows(d), rows(d), rows(width), rows(width), pl.BlockSpec((8, d), lambda i: (0, 0))],
        out_shape=[
            shape((tokens, d), WIDE),
            shape((tokens, d), LOW),
            shape((tokens, width), LOW),
            shape((tokens, width), LOW),
            shape((8, d), WIDE),
        ],
        compiler_params=params(),
        cost_estimate=cost(6),
        name="norm_back",
    )(mid, both, ga, gb, gain, w0, w1)


def together(*values):
    return lax.optimization_barrier(values)


def swap(value, axis, bits):
    size = lax.axis_size(axis)
    return lax.ppermute(value, axis, [(i, i ^ bits) for i in range(size)])


def has(axis, bit):
    return (lax.axis_index(axis) // bit) % 2 == 1


def in_order(flag, own, other, axis):
    return jnp.concatenate([jnp.where(flag, other, own), jnp.where(flag, own, other)], axis=axis)


def far_groups():
    at, groups = 2, []
    while at < lax.axis_size("dp"):
        size = min(4, lax.axis_size("dp") // at)
        groups.append((at, size))
        at *= size
    return groups


def far_place(group):
    at, size = group
    return (lax.axis_index("dp") // at) % size


def far_swaps(value, group):
    at, size = group
    return [swap(value, "dp", at * m) for m in range(1, size)]


def far_order(held, there, group):
    place, blocks = far_place(group), [held] + list(there)
    pick = lambda b: lax.select_n(place, *[blocks[b ^ p] for p in range(group[1])])
    return jnp.stack([pick(b) for b in range(group[1])])


def rows_of(held, there):
    return in_order(has("dp", 1), held[:, None], there[:, None], 1).reshape(-1, held.shape[-1])


def parted(grad):
    size = lax.axis_size("dp")
    parts = grad.reshape(size // 2, 2, grad.shape[0] // size, grad.shape[1])
    flag = has("dp", 1)
    return jnp.where(flag, parts[:, 1], parts[:, 0]), jnp.where(flag, parts[:, 0], parts[:, 1])


def added(a, b):
    return (a.astype(WIDE) + b.astype(WIDE)).astype(LOW)


class Gather:
    def __init__(self, piece):
        self.held, self.groups = piece[None], far_groups()
        while len(self.groups) > 1:
            self.far_start()
            self.far_end(self.there)

    def far_start(self):
        self.there = far_swaps(self.held, self.groups[0])

    def far_end(self, there):
        held = far_order(self.held, there, self.groups.pop(0))
        self.held = held.reshape((-1,) + held.shape[2:])

    def near_start(self):
        half = self.held.shape[-1] // 2
        self.a, self.b = self.held[..., :half], self.held[..., half:]
        self.there = swap(self.a, "dp", 1), swap(self.b, "tensor", 2)

    def near_end(self, there):
        self.a = rows_of(self.a, there[0])
        self.b = jnp.stack([self.b, there[1]])

    def last_start(self):
        self.there = swap(self.a, "tensor", 2), swap(self.b, "dp", 1)

    def last_end(self, there):
        b = [rows_of(self.b[i], there[1][i]) for i in (0, 1)]
        return (self.a, there[0]), b


class Scatter:
    def __init__(self, a0, a1, b0, b1):
        self.a_own, sent_own = parted(a0)
        self.a_other, sent_other = parted(a1)
        self.b = b0
        self.there = swap(jnp.stack([sent_own, sent_other]), "dp", 1), swap(b1, "tensor", 2)

    def near_end(self, there):
        self.a = added(self.a_own, there[0][0])
        self.b, sent = parted(added(self.b, there[1]))
        self.there = swap(added(self.a_other, there[0][1]), "tensor", 2), swap(sent, "dp", 1)

    def last_end(self, there):
        self.held = jnp.concatenate([added(self.a, there[0]), added(self.b, there[1])], axis=2)
        self.groups = far_groups()
        self.far_start()

    def far_start(self):
        at, size = self.groups[0]
        parts = self.held.reshape((-1, size) + self.held.shape[1:])
        place = far_place(self.groups[0])
        pick = lambda m: lax.dynamic_index_in_dim(parts, place ^ m, 1, keepdims=False)
        self.held = pick(0)
        self.there = [swap(pick(m), "dp", at * m) for m in range(1, size)]

    def far_end(self, there):
        total = self.held.astype(WIDE)
        for part in there:
            total = total + part.astype(WIDE)
        self.groups.pop(0)
        if not self.groups:
            return total[0]
        self.held = total.astype(LOW)
        self.far_start()
        return self.far_end(self.there)


def body(
    hidden, segment_ids, norm1_gain, norm1_bias, w_qkv, qv_bias, w_out, out_bias,
    norm2_gain, norm2_bias, w_up, up_bias, w_down, down_bias, cotangent,
):
    mine, d = hidden.shape
    width, units = w_qkv.shape[2], w_up.shape[1]
    half = units // 2
    core = has("tensor", 1)
    row = lambda v: v.reshape(1, -1)
    low_dot = lambda a, b: dot_first(a, b).astype(LOW)
    cat = lambda a, b: jnp.concatenate([a, b], axis=1)

    down = w_down.T
    g0 = Gather(jnp.concatenate([w_qkv[0], w_qkv[1], w_qkv[2], w_out.T], axis=1))
    g0.far_start()

    pair = jnp.concatenate([hidden, cotangent], axis=1)
    both = in_order(core, pair, swap(pair, "tensor", 1), 0)
    seg = lax.dynamic_index_in_dim(segment_ids, lax.axis_index("tensor") // 2, 0, keepdims=False)
    seg = seg.reshape(-1, 1)
    here = lax.axis_index("tensor") % 2 * mine
    there = mine - here
    biases = jnp.concatenate([qv_bias.reshape(-1), up_bias])
    other_biases = swap(biases, "tensor", 2)
    none = jnp.zeros((width,), WIDE)
    shift = jnp.stack(
        [jnp.concatenate([v[:width], none, v[width : 2 * width]]) for v in (biases, other_biases)]
    )
    scale = jnp.concatenate([none + HEAD_DIM ** (-0.5), none + 1.0, none + 1.0]).reshape(1, -1)
    chunk1 = jnp.concatenate([w_up[:, :half], down[:, :half]], axis=1)
    chunk2 = jnp.concatenate([w_up[:, half:], down[:, half:]], axis=1)

    swaps, both, shift, chunk1, chunk2 = together(g0.there, both, shift, chunk1, chunk2)
    g0.far_end(swaps)
    g0.near_start()
    g1 = Gather(chunk1)
    g1.far_start()
    (swaps,) = together(g0.there)
    g0.near_end(swaps)
    g0.last_start()
    swaps, swaps1 = together(g0.there, g1.there)
    (a0, a1), (b0, b1) = g0.last_end(swaps)
    w0, w1 = cat(a0, b0), cat(a1, b1)
    g1.far_end(swaps1)
    g1.near_start()
    n1, p0, p1 = project(both, row(norm1_gain), row(norm1_bias), w0, w1, shift, scale)
    swaps, n1, p0, p1, chunk2 = together(g1.there, n1, p0, p1, chunk2)
    g1.near_end(swaps)
    g1.last_start()
    g2 = Gather(chunk2)
    g2.far_start()
    att1, log1 = attend(p1, seg)
    att0, log0 = attend(p0, seg)
    swaps, swaps2, att0, log0, att1, log1 = together(g1.there, g2.there, att0, log0, att1, log1)
    (up0, up1), (dn0, dn1) = g1.last_end(swaps)
    g2.far_end(swaps2)
    g2.near_start()
    cut = w0.shape[1] - att0.shape[1]
    pa = (dot_last(att0, w0[:, cut:]) + dot_last(att1, w1[:, cut:])).astype(LOW)
    pb = swap(pa, "tensor", 1)
    unit_bias = lambda at: row(jnp.concatenate([up_bias[at : at + half], other_biases[2 * width + at :][:half]]))
    swaps, pa, pb = together(g2.there, pa, pb)
    g2.near_end(swaps)
    g2.last_start()
    act1, gu1, mlp, ga, units1, middle, n2 = mlp_pass(
        True, both, both, (pa, pb, row(out_bias), row(norm2_gain), row(norm2_bias)),
        unit_bias(0), cat(up0, up1), cat(dn0, dn1),
    )
    cot_all = both[:, d:]
    u, v = low_dot(n2, gu1), low_dot(cot_all, act1)
    swaps, u, v, mlp, ga, middle, n2 = together(g2.there, u, v, mlp, ga, middle, n2)
    (up0, up1), (dn0, dn1) = g2.last_end(swaps)
    s1 = Scatter(u[:, :half], u[:, half:], v[:, :half], v[:, half:])
    act2, gu2, mlp, ga, units2 = mlp_pass(
        False, n2, both, (mlp, ga), unit_bias(half), cat(up0, up1), cat(dn0, dn1)
    )
    swaps, act2, gu2, mlp, ga = together(s1.there, act2, gu2, mlp, ga)
    gb = swap(ga, "tensor", 1)
    s1.near_end(swaps)
    u, v = low_dot(n2, gu2), low_dot(cot_all, act2)
    swaps, u, v, ga, gb = together(s1.there, u, v, ga, gb)
    s2 = Scatter(u[:, :half], u[:, half:], v[:, :half], v[:, half:])
    s1.last_end(swaps)
    grad_mid, grad_attn, gatt0, gatt1, sums = norm_back(
        middle, both, ga, gb, row(norm2_gain), w0, w1, att0.shape[1]
    )
    gp1, gsum1 = attend_back(p1, seg, att1, log1, gatt1)
    swaps, swaps1, gp1, gsum1, gatt0 = together(s2.there, s1.there, gp1, gsum1, gatt0)
    s2.near_end(swaps)
    grad1 = s1.far_end(swaps1)
    gp0, gsum0 = attend_back(p0, seg, att0, log0, gatt0)
    front = [low_dot(n1, gp) for gp in (gp0, gp1)]
    tail = [low_dot(grad_attn, att[:, HEAD_DIM:]) for att in (att0, att1)]
    swaps, gp0, gsum0, front, tail = together(s2.there, gp0, gsum0, front, tail)
    s0 = Scatter(
        front[0][:, : 2 * width], front[1][:, : 2 * width],
        cat(front[0][:, 2 * width :], tail[0]), cat(front[1][:, 2 * width :], tail[1]),
    )
    s2.last_end(swaps)

    def branch(start):
        cut_rows = lambda v: lax.dynamic_slice_in_dim(v, start, mine, 0)
        return dot_last(cut_rows(gp0), w0[:, : 3 * width]) + dot_last(cut_rows(gp1), w1[:, : 3 * width])

    from_there = swap(branch(there).astype(LOW), "tensor", 1)
    grad_normed1 = branch(here) + from_there.astype(WIDE)

    center, inverse = centered(hidden.astype(WIDE))
    normal = center * inverse
    f = grad_normed1 * norm1_gain
    grad_input = inverse * (f - jnp.mean(f, -1, keepdims=True) - normal * jnp.mean(f * normal, -1, keepdims=True))
    grad_hidden = (lax.dynamic_slice_in_dim(grad_mid, here, mine, 0) + grad_input).astype(LOW)
    norm1_sums = jnp.stack([jnp.sum(grad_normed1 * normal, 0), jnp.sum(grad_normed1, 0)])
    norm1_sums = norm1_sums + swap(norm1_sums, "tensor", 1)
    shared = jnp.concatenate([norm1_sums.reshape(-1), sums[:4].reshape(-1)])
    part = lambda gsum, at: jnp.concatenate(
        [gsum[0, :width], gsum[0, 2 * width :], units1[0, at : at + half], units2[0, at : at + half]]
    )

    mlp_there = swap(lax.dynamic_slice_in_dim(mlp, there, mine, 0), "tensor", 1)
    mlp_here = lax.dynamic_slice_in_dim(mlp, here, mine, 0)
    output = lax.dynamic_slice_in_dim(middle, here, mine, 0) + down_bias
    output = (output + (mlp_here.astype(WIDE) + mlp_there.astype(WIDE))).astype(LOW)

    swaps, swaps2, grad_hidden, output, shared = together(s0.there, s2.there, grad_hidden, output, shared)
    own, other = part(gsum0, 0), part(gsum1, half)
    sent = jnp.concatenate([shared, own, other])
    over_x = swap(sent, "dp", 1)
    over_y, over_both = swap(sent, "tensor", 2), lax.ppermute(
        sent, ("dp", "tensor"),
        [
            (i * lax.axis_size("tensor") + t, (i ^ 1) * lax.axis_size("tensor") + (t ^ 2))
            for i in range(lax.axis_size("dp"))
            for t in range(lax.axis_size("tensor"))
        ],
    )
    over_x, over_y, over_both = together(over_x, over_y, over_both)
    s0.near_end(swaps)
    grad2 = s2.far_end(swaps2)
    full, units_here = 6 * d, 2 * width + units
    total = (sent + over_x)[: full + units_here]
    flipped = over_y + over_both
    total = total + jnp.concatenate([flipped[:full], flipped[full + units_here :]])
    swaps, total, grad2 = together(s0.there, total, grad2)
    for group in far_groups():
        total = sum(far_swaps(total, group), total)
    s0.last_end(swaps)
    swaps, total = together(s0.there, total)
    grad0 = s0.far_end(swaps)
    norm1_gain_grad, norm1_bias_grad, gain2, bias2, out_grad, down_grad = (
        total[i * d : (i + 1) * d] for i in range(6)
    )
    own = total[full:]
    columns = lambda i: grad0[:, i * width : (i + 1) * width]
    return (
        output,
        grad_hidden,
        norm1_gain_grad,
        norm1_bias_grad,
        jnp.stack([columns(0), columns(1), columns(2)]),
        own[: 2 * width].reshape(2, width),
        columns(3).T,
        out_grad,
        gain2,
        bias2,
        cat(grad1[:, :half], grad2[:, :half]),
        own[2 * width :],
        cat(grad1[:, half:], grad2[:, half:]).T,
        down_grad,
    )


def solution(mesh):
    placed = (
        P(("dp", "tensor"), None),
        P("dp", None),
        P(),
        P(),
        P(None, "dp", "tensor"),
        P(None, "tensor"),
        P("tensor", "dp"),
        P(),
        P(),
        P(),
        P("dp", "tensor"),
        P("tensor"),
        P("tensor", "dp"),
        P(),
        P(("dp", "tensor"), None),
    )
    return jax.shard_map(
        body,
        mesh=mesh,
        in_specs=placed,
        out_specs=(
            P(("dp", "tensor"), None),
            P(("dp", "tensor"), None),
            P(),
            P(),
            P(None, "dp", "tensor"),
            P(None, "tensor"),
            P("tensor", "dp"),
            P(),
            P(),
            P(),
            P("dp", "tensor"),
            P("tensor"),
            P("tensor", "dp"),
            P(),
        ),
        check_vma=False,
    )
```

```python
from functools import partial

import jax
import jax.numpy as jnp
from jax import lax
from jax.experimental import pallas as pl
from jax.experimental.pallas import tpu as pltpu
from jax.sharding import PartitionSpec as P

HEAD_DIM = 64
BLOCK = 256
UNIT_BLOCK = 512
LOW = jnp.bfloat16
WIDE = jnp.float32
BLOCKED = -1e30


def dot(a, b):
    return jnp.dot(a, b, preferred_element_type=WIDE)


def dot_last(a, b):
    return lax.dot_general(a, b, (((1,), (1,)), ((), ())), preferred_element_type=WIDE)


def dot_first(a, b):
    return lax.dot_general(a, b, (((0,), (0,)), ((), ())), preferred_element_type=WIDE)


def far(shapes):
    return [pltpu.HBM(s.shape, s.dtype) for s in shapes]


def hbm(value):
    return pltpu.with_memory_space_constraint(value, pltpu.HBM)


def params(megabytes=56):
    return pltpu.CompilerParams(vmem_limit_bytes=megabytes * 1024 * 1024)


def cost(micros):
    return pl.CostEstimate(flops=int(micros * 1.15e9), bytes_accessed=0, transcendentals=0)


def gated(kernel, reads, gates):
    return lambda *refs: kernel(*refs[:reads], *refs[reads + len(gates) :])


def gate_specs(gates):
    return [pl.BlockSpec(memory_space=pl.ANY)] * len(gates)


def centered(values):
    center = values - jnp.mean(values, -1, keepdims=True)
    spread = jnp.mean(center * center, -1, keepdims=True)
    return center, lax.rsqrt(spread + 1e-05)


def place_rows(target, held, there, flag):
    for block in range(held.shape[0]):
        target[2 * block + flag] = held[block]
        target[2 * block + 1 - flag] = there[block]


def project_kernel(
    flag_ref, x_ref, gain_ref, bias_ref, a0_ref, a1_ref, held_ref, there_ref, shift_ref, scale_ref,
    n_ref, p0_ref, p1_ref, w0_ref, w1_ref, rows_ref,
):
    half = a0_ref.shape[1]

    @pl.when(pl.program_id(0) == 0)
    def _():
        for number, (a_ref, w_ref) in enumerate(((a0_ref, w0_ref), (a1_ref, w1_ref))):
            w_ref[:, :half] = a_ref[...]
            place_rows(rows_ref, held_ref.at[number], there_ref.at[number], flag_ref[0])
            w_ref[:, half:] = rows_ref[...].reshape(w_ref.shape[0], half)

    center, inverse = centered(x_ref[...].astype(WIDE))
    normed = (center * inverse * gain_ref[...] + bias_ref[...]).astype(LOW)
    n_ref[...] = normed
    width = p0_ref.shape[1]
    for number, (w_ref, p_ref) in enumerate(((w0_ref, p0_ref), (w1_ref, p1_ref))):
        proj = dot(normed, w_ref[:, :width])
        p_ref[...] = ((proj + shift_ref[number : number + 1]) * scale_ref[...]).astype(LOW)


def project(flag, both, gain, bias, a0, a1, held, there, shift, scale):
    tokens, d = both.shape[0], a0.shape[0]
    width, half = shift.shape[1], a0.shape[1]
    whole = lambda a: pl.BlockSpec(a.shape, lambda i: (0,) * a.ndim, pipeline_mode=pl.Buffered(1))
    rows = lambda n: pl.BlockSpec((BLOCK, n), lambda i: (i, 0))
    shape = jax.ShapeDtypeStruct
    weight = shape((d, 2 * half), LOW)
    return pl.pallas_call(
        project_kernel,
        grid=(tokens // BLOCK,),
        in_specs=[pl.BlockSpec(memory_space=pltpu.SMEM), rows(d)]
        + [whole(a) for a in (gain, bias, a0, a1, held, there, shift, scale)],
        out_specs=[rows(d), rows(width), rows(width), whole(weight), whole(weight)],
        out_shape=[
            shape((tokens, d), LOW),
            shape((tokens, width), LOW),
            shape((tokens, width), LOW),
            weight,
            weight,
        ],
        scratch_shapes=[pltpu.VMEM((2 * held.shape[1], held.shape[2], half), LOW)],
        compiler_params=params(16),
        cost_estimate=cost(5),
        name="project",
    )(flag, both, gain, bias, a0, a1, held, there, shift, scale)


def features(seg, heads_values, blocked):
    lane = lax.broadcasted_iota(jnp.int32, (seg.shape[0], HEAD_DIM), 1)
    same = lane == seg
    if blocked:
        extra = jnp.where(same | (lane > 3), 0.0, BLOCKED)
    else:
        extra = jnp.where(same, 1.0, 0.0)
    return jnp.concatenate([heads_values, extra.astype(LOW)], axis=1)


def causal(scores_t):
    key = lax.broadcasted_iota(jnp.int32, scores_t.shape, 0)
    query = lax.broadcasted_iota(jnp.int32, scores_t.shape, 1)
    return jnp.where(key <= query, scores_t, BLOCKED)


def attend_kernel(p_ref, seg_ref, out_ref, log_ref):
    length = p_ref.shape[0]
    heads = p_ref.shape[1] // (3 * HEAD_DIM)
    seg = seg_ref[...]
    logs = []
    outs = [jnp.zeros((length, HEAD_DIM), LOW)]
    for head in range(heads):
        at = lambda c: slice((c * heads + head) * HEAD_DIM, (c * heads + head + 1) * HEAD_DIM)
        query = features(seg, p_ref[:, at(0)], True)
        key = features(seg, p_ref[:, at(1)], False)
        value = p_ref[:, at(2)]
        head_logs, head_outs = [], []
        for block in range(length // BLOCK):
            start, stop = block * BLOCK, (block + 1) * BLOCK
            scores = dot_last(key[:stop], query[start:stop])
            last = causal(scores[start:])
            scores = last if block == 0 else jnp.concatenate([scores[:start], last], axis=0)
            top = jnp.max(scores, 0, keepdims=True)
            shifted = jnp.exp(scores - top)
            total = jnp.sum(shifted, 0, keepdims=True)
            result = dot_first(value[:stop], shifted.astype(LOW)) / total
            head_logs.append(top + jnp.log(total))
            head_outs.append(result.T.astype(LOW))
        logs.append(jnp.concatenate(head_logs, axis=1))
        outs.append(jnp.concatenate(head_outs, axis=0))
    out_ref[...] = jnp.concatenate(outs, axis=1)
    logs.append(jnp.zeros((8 - heads, length), WIDE))
    log_ref[...] = jnp.concatenate(logs, axis=0)


def attend(proj, seg, gates=()):
    length, width = proj.shape
    heads = width // (3 * HEAD_DIM)
    return pl.pallas_call(
        gated(attend_kernel, 2, gates),
        in_specs=[pl.BlockSpec(memory_space=pltpu.VMEM)] * 2 + gate_specs(gates),
        out_shape=[
            jax.ShapeDtypeStruct((length, (heads + 1) * HEAD_DIM), LOW),
            jax.ShapeDtypeStruct((8, length), WIDE),
        ],
        compiler_params=params(10),
        cost_estimate=cost(5.4),
        name="attend",
    )(proj, seg, *gates)


def attend_back_kernel(p_ref, seg_ref, out_ref, log_ref, grad_ref, gp_ref, sum_ref, dq_ref):
    length = p_ref.shape[0]
    heads = p_ref.shape[1] // (3 * HEAD_DIM)
    seg = seg_ref[...]
    pieces = [[], [], []]
    for head in range(heads):
        at = lambda c: slice((c * heads + head) * HEAD_DIM, (c * heads + head + 1) * HEAD_DIM)
        shifted_at = slice((head + 1) * HEAD_DIM, (head + 2) * HEAD_DIM)
        plain = p_ref[:, at(0)]
        query = features(seg, plain, True)
        plain_key = p_ref[:, at(1)]
        key = features(seg, plain_key, False)
        value = p_ref[:, at(2)]
        grad = grad_ref[:, shifted_at]
        log_row = log_ref[head : head + 1]
        product = grad.astype(WIDE) * out_ref[:, shifted_at].astype(WIDE)
        inner = jnp.sum(product.T, 0, keepdims=True)
        dks, dvs = [], []
        for block in range(length // BLOCK):
            start, stop = block * BLOCK, (block + 1) * BLOCK
            scores = dot_last(key[start:stop], query[start:])
            first = causal(scores[:, :BLOCK])
            if stop < length:
                first = jnp.concatenate([first, scores[:, BLOCK:]], axis=1)
            probs = jnp.exp(first - log_row[:, start:])
            grad_probs = dot_last(value[start:stop], grad[start:])
            grad_scores = (probs * (grad_probs - inner[:, start:])).astype(LOW)
            dvs.append(dot(probs.astype(LOW), grad[start:]).astype(LOW))
            dks.append(dot(grad_scores, plain[start:]).astype(LOW))
            part = dot_first(plain_key[start:stop], grad_scores)
            if block == 0:
                dq_ref[...] = part
            else:
                dq_ref[:, start:] += part
        dq = (dq_ref[...].T.astype(LOW).astype(WIDE) * HEAD_DIM ** (-0.5)).astype(LOW)
        pieces[0].append(dq)
        pieces[1].append(jnp.concatenate(dks, axis=0))
        pieces[2].append(jnp.concatenate(dvs, axis=0))
    grads = jnp.concatenate(pieces[0] + pieces[1] + pieces[2], axis=1)
    gp_ref[...] = grads
    sum_ref[...] = jnp.sum(grads.astype(WIDE), 0, keepdims=True)


def attend_back(proj, seg, out, logs, grad, gates=()):
    length, width = proj.shape
    heads = width // (3 * HEAD_DIM)
    return pl.pallas_call(
        gated(attend_back_kernel, 5, gates),
        in_specs=[pl.BlockSpec(memory_space=pltpu.VMEM)] * 5 + gate_specs(gates),
        out_shape=[
            jax.ShapeDtypeStruct((length, width), LOW),
            jax.ShapeDtypeStruct((1, width), WIDE),
        ],
        scratch_shapes=[pltpu.VMEM((HEAD_DIM, length), WIDE)],
        compiler_params=params(12),
        cost_estimate=cost(5.7),
        name="attend_back",
    )(proj, seg, out, logs, grad, *gates)


def mlp_kernel(opening, *refs):
    refs, (up_ref, dn_ref, rows_ref, up_sum_ref, dn_sum_ref) = refs[:-5], refs[-5:]
    if opening:
        flag_ref, x_ref, cot_ref, pa_ref, pb_ref, ob_ref, gain_ref, bias_ref = refs[:8]
        refs, (mid_ref, n_ref) = refs[8:-2], refs[-2:]
        middle = x_ref[...].astype(WIDE) + (pa_ref[...].astype(WIDE) + pb_ref[...].astype(WIDE)) + ob_ref[...]
        mid_ref[...] = middle
        center, inverse = centered(middle)
        normed = (center * inverse * gain_ref[...] + bias_ref[...]).astype(LOW)
        n_ref[...] = normed
        mlp = grad_normed = None
    else:
        flag_ref, n_ref, cot_ref, before_ref, grad_before_ref = refs[:5]
        refs = refs[5:]
        normed = n_ref[...]
        mlp, grad_normed = before_ref[...].astype(WIDE), grad_before_ref[...].astype(WIDE)
    ub_ref, up0_ref, up1_ref, held_ref, there_ref = refs[:5]
    mlp_ref, gn_ref, sum_ref, kept_ref, sent_ref, own_ref, other_ref = refs[5:]
    cot = cot_ref[...]
    width = up_ref.shape[1]
    half = width // 2
    chunk = 256
    step = pl.program_id(0)

    @pl.when(step == 0)
    def _():
        sum_ref[...] = jnp.zeros_like(sum_ref)
        up_sum_ref[...] = jnp.zeros_like(up_sum_ref)
        dn_sum_ref[...] = jnp.zeros_like(dn_sum_ref)
        up_ref[:, :half] = up0_ref[...]
        up_ref[:, half:] = up1_ref[...]
        for number in range(2):
            place_rows(rows_ref, held_ref.at[number], there_ref.at[number], flag_ref[0])
            dn_ref[:, number * half : (number + 1) * half] = rows_ref[...].reshape(dn_ref.shape[0], half)

    normed_t, cot_t = normed.T, cot.T
    for start in range(0, width, chunk):
        at = slice(start, start + chunk)
        upper = dot(normed, up_ref[:, at]) + ub_ref[:, at]
        grad_active = dot(cot, dn_ref[:, at])
        phi = 0.5 + 0.5 * lax.erf(upper * 0.5**0.5)
        density = jnp.exp(-0.5 * (upper * upper)) * 0.3989422804014327
        active = (upper * phi).astype(LOW)
        grad_upper = (grad_active * (phi + upper * density)).astype(LOW)
        sum_ref[:, at] += jnp.sum(grad_upper.astype(WIDE), 0, keepdims=True)
        up_sum_ref[:, at] += dot(normed_t, grad_upper)
        dn_sum_ref[:, at] += dot(cot_t, active)
        a = dot_last(active, dn_ref[:, at])
        b = dot_last(grad_upper, up_ref[:, at])
        mlp = a if mlp is None else mlp + a
        grad_normed = b if grad_normed is None else grad_normed + b
    mlp_ref[...] = mlp.astype(mlp_ref.dtype)
    gn_ref[...] = grad_normed.astype(gn_ref.dtype)

    @pl.when(step == pl.num_programs(0) - 1)
    def _():
        own_ref[...] = dn_sum_ref[:, :half].astype(LOW)
        other_ref[...] = dn_sum_ref[:, half:].astype(LOW)
        for number in range(2):
            columns = slice(number * half, (number + 1) * half)
            rows_ref[...] = up_sum_ref[:, columns].astype(LOW).reshape(rows_ref.shape)
            for block in range(kept_ref.shape[1]):
                kept_ref[number, block] = rows_ref[2 * block + flag_ref[0]]
                sent_ref[number, block] = rows_ref[2 * block + 1 - flag_ref[0]]


def mlp_pass(opening, flag, lead, both, others, up_bias, up0, up1, held, there, gates=()):
    tokens, d = both.shape[0], up0.shape[0]
    half = up0.shape[1]
    width = 2 * half
    whole = lambda a: pl.BlockSpec(a.shape, lambda i: (0,) * len(a.shape), pipeline_mode=pl.Buffered(1))
    once = lambda a: pl.BlockSpec(a.shape, lambda i: (0,) * len(a.shape))
    rows = lambda n: pl.BlockSpec((UNIT_BLOCK, n), lambda i: (i, 0))
    shape = jax.ShapeDtypeStruct
    spec_of = lambda a: rows(a.shape[1]) if a.shape[0] == tokens else whole(a)
    pair, side, sums = shape(held.shape, LOW), shape((d, half), LOW), shape((1, width), WIDE)
    out_specs = [rows(d), rows(d), once(sums), once(pair), once(pair), once(side), once(side)]
    out_shape = [shape((tokens, d), LOW), shape((tokens, d), LOW), sums, pair, pair, side, side]
    if opening:
        out_specs += [rows(d), rows(d)]
        out_shape += [shape((tokens, d), WIDE), shape((tokens, d), LOW)]
    return pl.pallas_call(
        gated(partial(mlp_kernel, opening), 8 + len(others), gates),
        grid=(tokens // UNIT_BLOCK,),
        in_specs=[pl.BlockSpec(memory_space=pltpu.SMEM), rows(d), pl.BlockSpec((UNIT_BLOCK, d), lambda i: (i, 1))]
        + [spec_of(a) for a in others]
        + [whole(a) for a in (up_bias, up0, up1, held, there)]
        + gate_specs(gates),
        out_specs=out_specs,
        out_shape=far(out_shape),
        scratch_shapes=[
            pltpu.VMEM((d, width), LOW),
            pltpu.VMEM((d, width), LOW),
            pltpu.VMEM((2 * held.shape[1], held.shape[2], half), LOW),
            pltpu.VMEM((d, width), WIDE),
            pltpu.VMEM((d, width), WIDE),
        ],
        compiler_params=params(44),
        cost_estimate=cost(12),
        name="mlp_first" if opening else "mlp_second",
    )(flag, hbm(lead), hbm(both), *[hbm(a) if a.shape[0] == tokens else a for a in others], up_bias, up0, up1, held, there, *gates)


def norm_back_kernel(mid_ref, cot_ref, ga_ref, gb_ref, gain_ref, w0_ref, w1_ref, gm_ref, low_ref, g0_ref, g1_ref, sum_ref):
    e = ga_ref[...].astype(WIDE) + gb_ref[...].astype(WIDE)
    cot = cot_ref[...].astype(WIDE)
    center, inverse = centered(mid_ref[...])
    normal = center * inverse
    f = e * gain_ref[...]
    grad = inverse * (f - jnp.mean(f, -1, keepdims=True) - normal * jnp.mean(f * normal, -1, keepdims=True))
    grad_mid = cot + grad
    gm_ref[...] = grad_mid
    low = grad_mid.astype(LOW)
    low_ref[...] = low
    split = w0_ref.shape[1] - g0_ref.shape[1]
    g0_ref[...] = dot(low, w0_ref[:, split:]).astype(LOW)
    g1_ref[...] = dot(low, w1_ref[:, split:]).astype(LOW)

    @pl.when(pl.program_id(0) == 0)
    def _():
        sum_ref[...] = jnp.zeros_like(sum_ref)

    for row, term in enumerate((e * normal, e, low.astype(WIDE), cot)):
        sum_ref[row : row + 1] += jnp.sum(term, 0, keepdims=True)


def norm_back(mid, both, ga, gb, gain, w0, w1, width, gates=()):
    tokens, d = mid.shape
    whole = lambda a: pl.BlockSpec(a.shape, lambda i: (0, 0), pipeline_mode=pl.Buffered(1))
    rows = lambda n: pl.BlockSpec((BLOCK, n), lambda i: (i, 0))
    shape = jax.ShapeDtypeStruct
    return pl.pallas_call(
        gated(norm_back_kernel, 7, gates),
        grid=(tokens // BLOCK,),
        in_specs=[rows(d), pl.BlockSpec((BLOCK, d), lambda i: (i, 1)), rows(d), rows(d)]
        + [whole(a) for a in (gain, w0, w1)]
        + gate_specs(gates),
        out_specs=[rows(d), rows(d), rows(width), rows(width), pl.BlockSpec((8, d), lambda i: (0, 0))],
        out_shape=far([
            shape((tokens, d), WIDE),
            shape((tokens, d), LOW),
            shape((tokens, width), LOW),
            shape((tokens, width), LOW),
            shape((8, d), WIDE),
        ]),
        compiler_params=params(18),
        cost_estimate=cost(6),
        name="norm_back",
    )(hbm(mid), hbm(both), hbm(ga), hbm(gb), gain, w0, w1, *gates)


def attention_grads_kernel(number, flag_ref, n_ref, grad_ref, gp_ref, att_ref, *refs):
    kept_ref, sent_ref, rest_ref, all_ref = refs[-4:]
    front = 2 * (gp_ref.shape[1] // 3)
    rows = kept_ref.shape[2]
    grads = dot_first(n_ref[...], gp_ref[...])
    tail = dot_first(grad_ref[...], att_ref[...])[:, HEAD_DIM:]
    rest_ref[...] = jnp.concatenate([grads[:, front:], tail], axis=1).astype(LOW)
    all_ref[...] = grads[:, :front].astype(LOW).reshape(all_ref.shape)
    flag = flag_ref[0]
    for block in range(kept_ref.shape[1]):
        kept_ref[0, block] = all_ref[2 * block + flag]
        sent_ref[0, block] = all_ref[2 * block + 1 - flag]


def attention_grads(number, flag, normed, grad, gp, att, before=()):
    d, size = normed.shape[1], lax.axis_size("dp")
    width = gp.shape[1] // 3
    shape = jax.ShapeDtypeStruct
    pair = shape((2, size // 2, d // size, 2 * width), LOW)
    pair_spec = pl.BlockSpec((1,) + pair.shape[1:], lambda i: (number, 0, 0, 0))
    whole = lambda a: pl.BlockSpec(a.shape, lambda i: (0, 0), pipeline_mode=pl.Buffered(1))
    return pl.pallas_call(
        partial(attention_grads_kernel, number),
        grid=(1,),
        in_specs=[pl.BlockSpec(memory_space=pltpu.SMEM)]
        + [whole(a) for a in (normed, grad, gp, att)]
        + [pl.BlockSpec(memory_space=pl.ANY)] * len(before),
        out_specs=[pair_spec, pair_spec, pl.BlockSpec((d, 2 * width), lambda i: (0, 0))],
        out_shape=[pair, pair, shape((d, 2 * width), LOW)],
        scratch_shapes=[pltpu.VMEM((size, d // size, 2 * width), LOW)],
        input_output_aliases={5: 0, 6: 1} if before else {},
        compiler_params=params(16),
        cost_estimate=cost(4),
        name="attention_grads",
    )(flag, normed, grad, gp, att, *before)


def together(*values):
    return lax.optimization_barrier(values)


def swap(value, axis, bits):
    size = lax.axis_size(axis)
    return lax.ppermute(value, axis, [(i, i ^ bits) for i in range(size)])


def has(axis, bit):
    return (lax.axis_index(axis) // bit) % 2 == 1


def cat(a, b):
    return jnp.concatenate([a, b], axis=1)


def in_order(flag, own, other, axis):
    return jnp.concatenate([jnp.where(flag, other, own), jnp.where(flag, own, other)], axis=axis)


def far_bits():
    bit, bits = lax.axis_size("dp") // 2, []
    while bit > 1:
        bits.append(bit)
        bit //= 2
    return bits


def far_groups():
    at, groups = 2, []
    while at < lax.axis_size("dp"):
        size = min(4, lax.axis_size("dp") // at)
        groups.append((at, size))
        at *= size
    return groups


def far_place(group):
    at, size = group
    return (lax.axis_index("dp") // at) % size


def far_swaps(value, group):
    at, size = group
    return [swap(value, "dp", at * m) for m in range(1, size)]


def far_order(held, there, group):
    place, blocks = far_place(group), [held] + list(there)
    pick = lambda b: lax.select_n(place, *[blocks[b ^ p] for p in range(group[1])])
    return jnp.stack([pick(b) for b in range(group[1])])


def rows_of(held, there):
    return in_order(has("dp", 1), held[:, None], there[:, None], 1).reshape(-1, held.shape[-1])


def parted(grad):
    size = lax.axis_size("dp")
    parts = grad.reshape(size // 2, 2, grad.shape[0] // size, grad.shape[1])
    flag = has("dp", 1)
    return jnp.where(flag, parts[:, 1], parts[:, 0]), jnp.where(flag, parts[:, 0], parts[:, 1])


def added(a, b):
    return (a.astype(WIDE) + b.astype(WIDE)).astype(LOW)


class Gather:
    def __init__(self, piece, parts, direct):
        self.held, self.parts, self.direct = piece[None], parts, direct
        self.steps = far_groups() if direct else far_bits()
        while len(self.steps) > (1 if direct else 2):
            self.far_start()
            self.far_end(self.there)

    def far_start(self):
        if self.direct:
            self.there = far_swaps(self.held, self.steps[0])
        else:
            self.there = swap(self.held, "dp", self.steps[0])

    def far_end(self, there):
        step = self.steps.pop(0)
        if self.direct:
            held = far_order(self.held, there, step)
        else:
            held = in_order(has("dp", step), self.held[:, None], there[:, None], 1)
        self.held = held.reshape((-1,) + held.shape[2:])

    def near_start(self):
        n = self.held.shape[-1] // (2 * self.parts)
        blocks = [self.held[..., i * n : (i + 1) * n] for i in range(2 * self.parts)]
        self.a, self.b = jnp.stack(blocks[: self.parts]), jnp.stack(blocks[self.parts :])
        self.there = swap(self.a, "dp", 1), swap(self.b, "tensor", 2)

    def near_end(self, there):
        self.a = [rows_of(a, x) for a, x in zip(self.a, there[0])]
        self.b = [jnp.stack([b, y]) for b, y in zip(self.b, there[1])]

    def last_start(self, part):
        self.there = swap(self.a[part], "tensor", 2), swap(self.b[part], "dp", 1)

    def last_end(self, part, there):
        return self.a[part], there[0], self.b[part], there[1]


class Scatter:
    def __init__(self):
        self.parts, self.extra = [], None

    def start(self, kept, sent, b_own, b_other):
        self.there = swap(sent, "dp", 1), swap(b_other, "tensor", 2)
        self.parts.append((kept, b_own))

    def near_end(self, part, there):
        kept, b_own = self.parts[part]
        b, b_sent = parted(added(b_own, there[1]))
        self.parts[part] = added(kept[0], there[0][0]), b, added(kept[1], there[0][1]), b_sent

    def last_start(self):
        self.a, self.b, sent_a, sent_b = (jnp.stack(v) for v in zip(*self.parts))
        self.sent = sent_a, sent_b
        self.there = swap(sent_a, "tensor", 2), swap(sent_b, "dp", 1)

    def last_end(self, there):
        a, b = added(self.a, there[0]), added(self.b, there[1])
        self.held = jnp.concatenate(list(a) + list(b), axis=2)
        self.groups = far_groups()
        self.far_start()

    def far_start(self):
        at, size = self.groups[0]
        parts = self.held.reshape((-1, size) + self.held.shape[1:])
        place = far_place(self.groups[0])
        pick = lambda m: lax.dynamic_index_in_dim(parts, place ^ m, 1, keepdims=False)
        self.held = pick(0)
        if self.extra is None:
            self.there = [swap(pick(m), "dp", at * m) for m in range(1, size)]
        else:
            high = lax.reduce_precision(self.extra, 8, 7)
            extra = [v.astype(LOW) for v in (high, self.extra - high)]
            n = self.held.shape[-1]
            self.there = [
                swap(jnp.concatenate([pick(m).reshape(-1, n)] + extra), "dp", at * m) for m in range(1, size)
            ]

    def far_end(self, there):
        total = self.held.astype(WIDE)
        rows = total.shape[0] * total.shape[1]
        for part in there:
            if self.extra is not None:
                high, low = jnp.split(part[rows:].astype(WIDE), 2)
                self.extra = self.extra + (high + low)
                part = part[:rows].reshape(total.shape)
            total = total + part.astype(WIDE)
        self.groups.pop(0)
        if not self.groups:
            return total[0]
        self.held = total.astype(LOW)
        self.far_start()
        return self.far_end(self.there)


def body(
    hidden, segment_ids, norm1_gain, norm1_bias, w_qkv, qv_bias, w_out, out_bias,
    norm2_gain, norm2_bias, w_up, up_bias, w_down, down_bias, cotangent,
):
    mine, d = hidden.shape
    width, units = w_qkv.shape[2], w_up.shape[1]
    half = units // 2
    core = has("tensor", 1)
    row = lambda v: v.reshape(1, -1)
    low_dot = lambda a, b: dot_first(a, b).astype(LOW)

    flag = has("dp", 1).astype(jnp.int32).reshape(1)

    g0 = Gather(jnp.concatenate([w_qkv[0], w_qkv[1], w_qkv[2], w_out.T], axis=1), 1, True)
    g0.far_start()
    units_piece = cat(w_up, w_down.T)

    pair = jnp.concatenate([hidden, cotangent], axis=1)
    both = in_order(core, pair, swap(pair, "tensor", 1), 0)
    seg = lax.dynamic_index_in_dim(segment_ids, lax.axis_index("tensor") // 2, 0, keepdims=False)
    seg = seg.reshape(-1, 1)
    here = lax.axis_index("tensor") % 2 * mine
    there = mine - here
    biases = jnp.concatenate([qv_bias.reshape(-1), up_bias])
    other_biases = swap(biases, "tensor", 2)
    none = jnp.zeros((width,), WIDE)
    shift = jnp.stack(
        [jnp.concatenate([v[:width], none, v[width : 2 * width]]) for v in (biases, other_biases)]
    )
    scale = jnp.concatenate([none + HEAD_DIM ** (-0.5), none + 1.0, none + 1.0]).reshape(1, -1)

    swaps, units_piece = together(g0.there, units_piece)
    g0.far_end(swaps)
    g0.near_start()
    g1 = Gather(units_piece, 2, False)
    g1.far_start()
    swaps, swaps1 = together(g0.there, g1.there)
    g0.near_end(swaps)
    g0.last_start(0)
    g1.far_end(swaps1)
    g1.far_start()
    swaps, swaps1 = together(g0.there, g1.there)
    g1.far_end(swaps1)
    g1.near_start()
    n1, p0, p1, w0, w1 = project(
        flag, both, row(norm1_gain), row(norm1_bias), *g0.last_end(0, swaps), shift, scale
    )
    att1, log1 = attend(p1, seg)
    swaps, log1 = together(g1.there, log1)
    g1.near_end(swaps)
    g1.last_start(0)
    att0, log0 = attend(p0, seg, (log1, g1.a[0], g1.b[0]))
    unit_bias = lambda at: row(jnp.concatenate([up_bias[at : at + half], other_biases[2 * width + at :][:half]]))
    swaps, log0, att0 = together(g1.there, log0, att0)
    cut = w0.shape[1] - att0.shape[1]
    pa = (dot_last(att0, w0[:, cut:]) + dot_last(att1, w1[:, cut:])).astype(LOW)
    pb = swap(pa, "tensor", 1)
    first_units = g1.last_end(0, swaps)
    g1.last_start(1)
    mlp, ga, units1, *grads, middle, n2 = mlp_pass(
        True, flag, both, both, (pa, pb, row(out_bias), row(norm2_gain), row(norm2_bias)),
        unit_bias(0), *first_units,
    )
    swaps, units1 = together(g1.there, units1)
    s1 = Scatter()
    s1.start(*grads)
    mlp, ga, units2, *grads = mlp_pass(
        False, flag, n2, both, (mlp, ga), unit_bias(half), *g1.last_end(1, swaps), (units1,)
    )
    kept, sent, own, other = grads
    swaps, units2, ga, sent, other = together(s1.there, units2, ga, sent, other)
    gb = swap(ga, "tensor", 1)
    s1.start(kept, sent, own, other)
    grad_mid, grad_attn, gatt0, gatt1, sums = norm_back(
        middle, both, ga, gb, row(norm2_gain), w0, w1, att0.shape[1], (units2,)
    )
    swaps, sums = together(swaps, sums)
    s1.near_end(0, swaps)
    gp1, gsum1 = attend_back(p1, seg, att1, log1, gatt1)
    swaps, gsum1 = together(s1.there, gsum1)
    s1.near_end(1, swaps)
    s1.last_start()
    kept, sent, last1 = attention_grads(1, flag, n1, grad_attn, gp1, att1)
    gp0, gsum0 = attend_back(p0, seg, att0, log0, gatt0, s1.sent + (gsum1,))
    kept, sent, last0 = attention_grads(0, flag, n1, grad_attn, gp0, att0, (kept, sent))
    swaps, gsum0, here, own_hidden, units1, units2 = together(s1.there, gsum0, here, hidden, units1, units2)
    there = mine - here
    s0 = Scatter()
    s0.start(kept, sent, last0, last1)
    s1.last_end(swaps)

    def branch(start):
        cut_rows = lambda v: lax.dynamic_slice_in_dim(v, start, mine, 0)
        return dot_last(cut_rows(gp0), w0[:, : 3 * width]) + dot_last(cut_rows(gp1), w1[:, : 3 * width])

    from_there = swap(branch(there).astype(LOW), "tensor", 1)
    grad_normed1 = branch(here) + from_there.astype(WIDE)

    center, inverse = centered(own_hidden.astype(WIDE))
    normal = center * inverse
    f = grad_normed1 * norm1_gain
    grad_input = inverse * (f - jnp.mean(f, -1, keepdims=True) - normal * jnp.mean(f * normal, -1, keepdims=True))
    grad_hidden = (lax.dynamic_slice_in_dim(grad_mid, here, mine, 0) + grad_input).astype(LOW)
    norm1_sums = jnp.stack([jnp.sum(grad_normed1 * normal, 0), jnp.sum(grad_normed1, 0)])
    norm1_sums = norm1_sums + swap(norm1_sums, "tensor", 1)
    shared = jnp.concatenate([norm1_sums.reshape(-1), sums[:4].reshape(-1)])
    part = lambda gsum, at: jnp.concatenate(
        [gsum[0, :width], gsum[0, 2 * width :], units1[0, at : at + half], units2[0, at : at + half]]
    )

    mlp_there = swap(lax.dynamic_slice_in_dim(mlp, there, mine, 0), "tensor", 1)
    mlp_here = lax.dynamic_slice_in_dim(mlp, here, mine, 0)
    output = lax.dynamic_slice_in_dim(middle, here, mine, 0) + down_bias
    output = (output + (mlp_here.astype(WIDE) + mlp_there.astype(WIDE))).astype(LOW)

    (swaps,) = together(s0.there)
    own, other = part(gsum0, 0), part(gsum1, half)
    s0.near_end(0, swaps)
    s0.last_start()
    sent = jnp.concatenate([shared, own, other])
    over_x = swap(sent, "dp", 1)
    over_y, over_both = swap(sent, "tensor", 2), lax.ppermute(
        sent, ("dp", "tensor"),
        [
            (i * lax.axis_size("tensor") + t, (i ^ 1) * lax.axis_size("tensor") + (t ^ 2))
            for i in range(lax.axis_size("dp"))
            for t in range(lax.axis_size("tensor"))
        ],
    )
    swaps, swaps1, over_x, over_y, over_both = together(s0.there, s1.there, over_x, over_y, over_both)
    full, units_here = 6 * d, 2 * width + units
    total = (sent + over_x)[: full + units_here]
    flipped = over_y + over_both
    total = total + jnp.concatenate([flipped[:full], flipped[full + units_here :]])
    s0.extra = jnp.pad(total, (0, -total.shape[0] % (8 * d))).reshape(-1, d)
    s0.last_end(swaps)
    grad1 = s1.far_end(swaps1)
    (swaps,) = together(s0.there)
    grad0 = s0.far_end(swaps)
    total = s0.extra.reshape(-1)[: total.shape[0]]
    norm1_gain_grad, norm1_bias_grad, gain2, bias2, out_grad, down_grad = (
        total[i * d : (i + 1) * d] for i in range(6)
    )
    own = total[full:]
    columns = lambda i: grad0[:, i * width : (i + 1) * width]
    return (
        output,
        grad_hidden,
        norm1_gain_grad,
        norm1_bias_grad,
        jnp.stack([columns(0), columns(1), columns(2)]),
        own[: 2 * width].reshape(2, width),
        columns(3).T,
        out_grad,
        gain2,
        bias2,
        grad1[:, :units],
        own[2 * width :],
        grad1[:, units:].T,
        down_grad,
    )


def solution(mesh):
    placed = (
        P(("dp", "tensor"), None),
        P("dp", None),
        P(),
        P(),
        P(None, "dp", "tensor"),
        P(None, "tensor"),
        P("tensor", "dp"),
        P(),
        P(),
        P(),
        P("dp", "tensor"),
        P("tensor"),
        P("tensor", "dp"),
        P(),
        P(("dp", "tensor"), None),
    )
    return jax.shard_map(
        body,
        mesh=mesh,
        in_specs=placed,
        out_specs=(
            P(("dp", "tensor"), None),
            P(("dp", "tensor"), None),
            P(),
            P(),
            P(None, "dp", "tensor"),
            P(None, "tensor"),
            P("tensor", "dp"),
            P(),
            P(),
            P(),
            P("dp", "tensor"),
            P("tensor"),
            P("tensor", "dp"),
            P(),
        ),
        check_vma=False,
    )
```

```python
from functools import partial

import jax
import jax.numpy as jnp
from jax import lax
from jax.experimental import pallas as pl
from jax.experimental.pallas import tpu as pltpu
from jax.sharding import PartitionSpec as P

HEAD_DIM = 64
BLOCK = 256
UNIT_BLOCK = 512
LOW = jnp.bfloat16
WIDE = jnp.float32
BLOCKED = -1e30


def dot(a, b):
    return jnp.dot(a, b, preferred_element_type=WIDE)


def dot_last(a, b):
    return lax.dot_general(a, b, (((1,), (1,)), ((), ())), preferred_element_type=WIDE)


def dot_first(a, b):
    return lax.dot_general(a, b, (((0,), (0,)), ((), ())), preferred_element_type=WIDE)


def far(shapes):
    return [pltpu.HBM(s.shape, s.dtype) for s in shapes]


def hbm(value):
    return pltpu.with_memory_space_constraint(value, pltpu.HBM)


def params(megabytes=56):
    return pltpu.CompilerParams(vmem_limit_bytes=megabytes * 1024 * 1024)


def cost(micros):
    return pl.CostEstimate(flops=int(micros * 1.15e9), bytes_accessed=0, transcendentals=0)


def gated(kernel, reads, gates):
    return lambda *refs: kernel(*refs[:reads], *refs[reads + len(gates) :])


def gate_specs(gates):
    return [pl.BlockSpec(memory_space=pl.ANY)] * len(gates)


def centered(values):
    center = values - jnp.mean(values, -1, keepdims=True)
    spread = jnp.mean(center * center, -1, keepdims=True)
    return center, lax.rsqrt(spread + 1e-05)


def place_rows(target, held, there, flag):
    for block in range(held.shape[0]):
        target[2 * block + flag] = held[block]
        target[2 * block + 1 - flag] = there[block]


def project_kernel(
    flag_ref, x_ref, gain_ref, bias_ref, a0_ref, a1_ref, held_ref, there_ref, shift_ref, scale_ref,
    n_ref, p0_ref, p1_ref, w0_ref, w1_ref, rows_ref,
):
    half = a0_ref.shape[1]

    @pl.when(pl.program_id(0) == 0)
    def _():
        for number, (a_ref, w_ref) in enumerate(((a0_ref, w0_ref), (a1_ref, w1_ref))):
            w_ref[:, :half] = a_ref[...]
            place_rows(rows_ref, held_ref.at[number], there_ref.at[number], flag_ref[0])
            w_ref[:, half:] = rows_ref[...].reshape(w_ref.shape[0], half)

    center, inverse = centered(x_ref[...].astype(WIDE))
    normed = (center * inverse * gain_ref[...] + bias_ref[...]).astype(LOW)
    n_ref[...] = normed
    width = p0_ref.shape[1]
    for number, (w_ref, p_ref) in enumerate(((w0_ref, p0_ref), (w1_ref, p1_ref))):
        proj = dot(normed, w_ref[:, :width])
        p_ref[...] = ((proj + shift_ref[number : number + 1]) * scale_ref[...]).astype(LOW)


def project(flag, both, gain, bias, a0, a1, held, there, shift, scale):
    tokens, d = both.shape[0], a0.shape[0]
    width, half = shift.shape[1], a0.shape[1]
    whole = lambda a: pl.BlockSpec(a.shape, lambda i: (0,) * a.ndim, pipeline_mode=pl.Buffered(1))
    rows = lambda n: pl.BlockSpec((BLOCK, n), lambda i: (i, 0))
    shape = jax.ShapeDtypeStruct
    weight = shape((d, 2 * half), LOW)
    return pl.pallas_call(
        project_kernel,
        grid=(tokens // BLOCK,),
        in_specs=[pl.BlockSpec(memory_space=pltpu.SMEM), rows(d)]
        + [whole(a) for a in (gain, bias, a0, a1, held, there, shift, scale)],
        out_specs=[rows(d), rows(width), rows(width), whole(weight), whole(weight)],
        out_shape=[
            shape((tokens, d), LOW),
            shape((tokens, width), LOW),
            shape((tokens, width), LOW),
            weight,
            weight,
        ],
        scratch_shapes=[pltpu.VMEM((2 * held.shape[1], held.shape[2], half), LOW)],
        compiler_params=params(16),
        cost_estimate=cost(5),
        name="project",
    )(flag, both, gain, bias, a0, a1, held, there, shift, scale)


def features(seg, heads_values, blocked):
    lane = lax.broadcasted_iota(jnp.int32, (seg.shape[0], HEAD_DIM), 1)
    same = lane == seg
    if blocked:
        extra = jnp.where(same | (lane > 3), 0.0, BLOCKED)
    else:
        extra = jnp.where(same, 1.0, 0.0)
    return jnp.concatenate([heads_values, extra.astype(LOW)], axis=1)


def causal(scores_t):
    key = lax.broadcasted_iota(jnp.int32, scores_t.shape, 0)
    query = lax.broadcasted_iota(jnp.int32, scores_t.shape, 1)
    return jnp.where(key <= query, scores_t, BLOCKED)


def attend_kernel(p_ref, seg_ref, out_ref, log_ref):
    length = p_ref.shape[0]
    heads = p_ref.shape[1] // (3 * HEAD_DIM)
    seg = seg_ref[...]
    logs = []
    outs = [jnp.zeros((length, HEAD_DIM), LOW)]
    for head in range(heads):
        at = lambda c: slice((c * heads + head) * HEAD_DIM, (c * heads + head + 1) * HEAD_DIM)
        query = features(seg, p_ref[:, at(0)], True)
        key = features(seg, p_ref[:, at(1)], False)
        value = p_ref[:, at(2)]
        head_logs, head_outs = [], []
        for block in range(length // BLOCK):
            start, stop = block * BLOCK, (block + 1) * BLOCK
            scores = dot_last(key[:stop], query[start:stop])
            last = causal(scores[start:])
            scores = last if block == 0 else jnp.concatenate([scores[:start], last], axis=0)
            top = jnp.max(scores, 0, keepdims=True)
            shifted = jnp.exp(scores - top)
            total = jnp.sum(shifted, 0, keepdims=True)
            result = dot_first(value[:stop], shifted.astype(LOW)) / total
            head_logs.append(top + jnp.log(total))
            head_outs.append(result.T.astype(LOW))
        logs.append(jnp.concatenate(head_logs, axis=1))
        outs.append(jnp.concatenate(head_outs, axis=0))
    out_ref[...] = jnp.concatenate(outs, axis=1)
    logs.append(jnp.zeros((8 - heads, length), WIDE))
    log_ref[...] = jnp.concatenate(logs, axis=0)


def attend(proj, seg, gates=()):
    length, width = proj.shape
    heads = width // (3 * HEAD_DIM)
    return pl.pallas_call(
        gated(attend_kernel, 2, gates),
        in_specs=[pl.BlockSpec(memory_space=pltpu.VMEM)] * 2 + gate_specs(gates),
        out_shape=[
            jax.ShapeDtypeStruct((length, (heads + 1) * HEAD_DIM), LOW),
            jax.ShapeDtypeStruct((8, length), WIDE),
        ],
        compiler_params=params(10),
        cost_estimate=cost(5.4),
        name="attend",
    )(proj, seg, *gates)


def attend_back_kernel(p_ref, seg_ref, out_ref, log_ref, grad_ref, gp_ref, sum_ref, dq_ref):
    length = p_ref.shape[0]
    heads = p_ref.shape[1] // (3 * HEAD_DIM)
    seg = seg_ref[...]
    pieces = [[], [], []]
    for head in range(heads):
        at = lambda c: slice((c * heads + head) * HEAD_DIM, (c * heads + head + 1) * HEAD_DIM)
        shifted_at = slice((head + 1) * HEAD_DIM, (head + 2) * HEAD_DIM)
        plain = p_ref[:, at(0)]
        query = features(seg, plain, True)
        plain_key = p_ref[:, at(1)]
        key = features(seg, plain_key, False)
        value = p_ref[:, at(2)]
        grad = grad_ref[:, shifted_at]
        log_row = log_ref[head : head + 1]
        product = grad.astype(WIDE) * out_ref[:, shifted_at].astype(WIDE)
        inner = jnp.sum(product.T, 0, keepdims=True)
        dks, dvs = [], []
        for block in range(length // BLOCK):
            start, stop = block * BLOCK, (block + 1) * BLOCK
            scores = dot_last(key[start:stop], query[start:])
            first = causal(scores[:, :BLOCK])
            if stop < length:
                first = jnp.concatenate([first, scores[:, BLOCK:]], axis=1)
            probs = jnp.exp(first - log_row[:, start:])
            grad_probs = dot_last(value[start:stop], grad[start:])
            grad_scores = (probs * (grad_probs - inner[:, start:])).astype(LOW)
            dvs.append(dot(probs.astype(LOW), grad[start:]).astype(LOW))
            dks.append(dot(grad_scores, plain[start:]).astype(LOW))
            part = dot_first(plain_key[start:stop], grad_scores)
            if block == 0:
                dq_ref[...] = part
            else:
                dq_ref[:, start:] += part
        dq = (dq_ref[...].T.astype(LOW).astype(WIDE) * HEAD_DIM ** (-0.5)).astype(LOW)
        pieces[0].append(dq)
        pieces[1].append(jnp.concatenate(dks, axis=0))
        pieces[2].append(jnp.concatenate(dvs, axis=0))
    grads = jnp.concatenate(pieces[0] + pieces[1] + pieces[2], axis=1)
    gp_ref[...] = grads
    sum_ref[...] = jnp.sum(grads.astype(WIDE), 0, keepdims=True)


def attend_back(proj, seg, out, logs, grad, gates=()):
    length, width = proj.shape
    heads = width // (3 * HEAD_DIM)
    return pl.pallas_call(
        gated(attend_back_kernel, 5, gates),
        in_specs=[pl.BlockSpec(memory_space=pltpu.VMEM)] * 5 + gate_specs(gates),
        out_shape=[
            jax.ShapeDtypeStruct((length, width), LOW),
            jax.ShapeDtypeStruct((1, width), WIDE),
        ],
        scratch_shapes=[pltpu.VMEM((HEAD_DIM, length), WIDE)],
        compiler_params=params(12),
        cost_estimate=cost(5.7),
        name="attend_back",
    )(proj, seg, out, logs, grad, *gates)


def mlp_kernel(opening, *refs):
    refs, (up_ref, dn_ref, rows_ref, up_sum_ref, dn_sum_ref) = refs[:-5], refs[-5:]
    if opening:
        flag_ref, x_ref, cot_ref, pa_ref, pb_ref, ob_ref, gain_ref, bias_ref = refs[:8]
        refs, (mid_ref, n_ref) = refs[8:-2], refs[-2:]
        middle = x_ref[...].astype(WIDE) + (pa_ref[...].astype(WIDE) + pb_ref[...].astype(WIDE)) + ob_ref[...]
        mid_ref[...] = middle
        center, inverse = centered(middle)
        normed = (center * inverse * gain_ref[...] + bias_ref[...]).astype(LOW)
        n_ref[...] = normed
        mlp = grad_normed = None
    else:
        flag_ref, n_ref, cot_ref, before_ref, grad_before_ref = refs[:5]
        refs = refs[5:]
        normed = n_ref[...]
        mlp, grad_normed = before_ref[...].astype(WIDE), grad_before_ref[...].astype(WIDE)
    ub_ref, up0_ref, up1_ref, held_ref, there_ref = refs[:5]
    mlp_ref, gn_ref, sum_ref, kept_ref, sent_ref, own_ref, other_ref = refs[5:]
    cot = cot_ref[...]
    width = up_ref.shape[1]
    half = width // 2
    chunk = 256
    step = pl.program_id(0)

    @pl.when(step == 0)
    def _():
        sum_ref[...] = jnp.zeros_like(sum_ref)
        up_sum_ref[...] = jnp.zeros_like(up_sum_ref)
        dn_sum_ref[...] = jnp.zeros_like(dn_sum_ref)
        up_ref[:, :half] = up0_ref[...]
        up_ref[:, half:] = up1_ref[...]
        for number in range(2):
            place_rows(rows_ref, held_ref.at[number], there_ref.at[number], flag_ref[0])
            dn_ref[:, number * half : (number + 1) * half] = rows_ref[...].reshape(dn_ref.shape[0], half)

    normed_t, cot_t = normed.T, cot.T
    for start in range(0, width, chunk):
        at = slice(start, start + chunk)
        upper = dot(normed, up_ref[:, at]) + ub_ref[:, at]
        grad_active = dot(cot, dn_ref[:, at])
        phi = 0.5 + 0.5 * lax.erf(upper * 0.5**0.5)
        density = jnp.exp(-0.5 * (upper * upper)) * 0.3989422804014327
        active = (upper * phi).astype(LOW)
        grad_upper = (grad_active * (phi + upper * density)).astype(LOW)
        sum_ref[:, at] += jnp.sum(grad_upper.astype(WIDE), 0, keepdims=True)
        up_sum_ref[:, at] += dot(normed_t, grad_upper)
        dn_sum_ref[:, at] += dot(cot_t, active)
        a = dot_last(active, dn_ref[:, at])
        b = dot_last(grad_upper, up_ref[:, at])
        mlp = a if mlp is None else mlp + a
        grad_normed = b if grad_normed is None else grad_normed + b
    mlp_ref[...] = mlp.astype(mlp_ref.dtype)
    gn_ref[...] = grad_normed.astype(gn_ref.dtype)

    @pl.when(step == pl.num_programs(0) - 1)
    def _():
        own_ref[...] = dn_sum_ref[:, :half].astype(LOW)
        other_ref[...] = dn_sum_ref[:, half:].astype(LOW)
        for number in range(2):
            columns = slice(number * half, (number + 1) * half)
            rows_ref[...] = up_sum_ref[:, columns].astype(LOW).reshape(rows_ref.shape)
            for block in range(kept_ref.shape[1]):
                kept_ref[number, block] = rows_ref[2 * block + flag_ref[0]]
                sent_ref[number, block] = rows_ref[2 * block + 1 - flag_ref[0]]


def mlp_pass(opening, flag, lead, both, others, up_bias, up0, up1, held, there, gates=()):
    tokens, d = both.shape[0], up0.shape[0]
    half = up0.shape[1]
    width = 2 * half
    whole = lambda a: pl.BlockSpec(a.shape, lambda i: (0,) * len(a.shape), pipeline_mode=pl.Buffered(1))
    once = lambda a: pl.BlockSpec(a.shape, lambda i: (0,) * len(a.shape))
    rows = lambda n: pl.BlockSpec((UNIT_BLOCK, n), lambda i: (i, 0))
    shape = jax.ShapeDtypeStruct
    spec_of = lambda a: rows(a.shape[1]) if a.shape[0] == tokens else whole(a)
    pair, side, sums = shape(held.shape, LOW), shape((d, half), LOW), shape((1, width), WIDE)
    out_specs = [rows(d), rows(d), once(sums), once(pair), once(pair), once(side), once(side)]
    out_shape = [shape((tokens, d), LOW), shape((tokens, d), LOW), sums, pair, pair, side, side]
    if opening:
        out_specs += [rows(d), rows(d)]
        out_shape += [shape((tokens, d), WIDE), shape((tokens, d), LOW)]
    return pl.pallas_call(
        gated(partial(mlp_kernel, opening), 8 + len(others), gates),
        grid=(tokens // UNIT_BLOCK,),
        in_specs=[pl.BlockSpec(memory_space=pltpu.SMEM), rows(d), pl.BlockSpec((UNIT_BLOCK, d), lambda i: (i, 1))]
        + [spec_of(a) for a in others]
        + [whole(a) for a in (up_bias, up0, up1, held, there)]
        + gate_specs(gates),
        out_specs=out_specs,
        out_shape=far(out_shape),
        scratch_shapes=[
            pltpu.VMEM((d, width), LOW),
            pltpu.VMEM((d, width), LOW),
            pltpu.VMEM((2 * held.shape[1], held.shape[2], half), LOW),
            pltpu.VMEM((d, width), WIDE),
            pltpu.VMEM((d, width), WIDE),
        ],
        compiler_params=params(44),
        cost_estimate=cost(12),
        name="mlp_first" if opening else "mlp_second",
    )(flag, hbm(lead), hbm(both), *[hbm(a) if a.shape[0] == tokens else a for a in others], up_bias, up0, up1, held, there, *gates)


def norm_back_kernel(mid_ref, cot_ref, ga_ref, gb_ref, gain_ref, w0_ref, w1_ref, gm_ref, low_ref, g0_ref, g1_ref, sum_ref):
    e = ga_ref[...].astype(WIDE) + gb_ref[...].astype(WIDE)
    cot = cot_ref[...].astype(WIDE)
    center, inverse = centered(mid_ref[...])
    normal = center * inverse
    f = e * gain_ref[...]
    grad = inverse * (f - jnp.mean(f, -1, keepdims=True) - normal * jnp.mean(f * normal, -1, keepdims=True))
    grad_mid = cot + grad
    gm_ref[...] = grad_mid
    low = grad_mid.astype(LOW)
    low_ref[...] = low
    split = w0_ref.shape[1] - g0_ref.shape[1]
    g0_ref[...] = dot(low, w0_ref[:, split:]).astype(LOW)
    g1_ref[...] = dot(low, w1_ref[:, split:]).astype(LOW)

    @pl.when(pl.program_id(0) == 0)
    def _():
        sum_ref[...] = jnp.zeros_like(sum_ref)

    for row, term in enumerate((e * normal, e, low.astype(WIDE), cot)):
        sum_ref[row : row + 1] += jnp.sum(term, 0, keepdims=True)


def norm_back(mid, both, ga, gb, gain, w0, w1, width, gates=()):
    tokens, d = mid.shape
    whole = lambda a: pl.BlockSpec(a.shape, lambda i: (0, 0), pipeline_mode=pl.Buffered(1))
    rows = lambda n: pl.BlockSpec((UNIT_BLOCK, n), lambda i: (i, 0))
    shape = jax.ShapeDtypeStruct
    return pl.pallas_call(
        gated(norm_back_kernel, 7, gates),
        grid=(tokens // UNIT_BLOCK,),
        in_specs=[rows(d), pl.BlockSpec((UNIT_BLOCK, d), lambda i: (i, 1)), rows(d), rows(d)]
        + [whole(a) for a in (gain, w0, w1)]
        + gate_specs(gates),
        out_specs=[rows(d), rows(d), rows(width), rows(width), pl.BlockSpec((8, d), lambda i: (0, 0))],
        out_shape=far([
            shape((tokens, d), WIDE),
            shape((tokens, d), LOW),
            shape((tokens, width), LOW),
            shape((tokens, width), LOW),
            shape((8, d), WIDE),
        ]),
        compiler_params=params(30),
        cost_estimate=cost(6),
        name="norm_back",
    )(hbm(mid), hbm(both), hbm(ga), hbm(gb), gain, w0, w1, *gates)


def attention_grads_kernel(number, flag_ref, n_ref, grad_ref, gp_ref, att_ref, *refs):
    kept_ref, sent_ref, rest_ref, all_ref = refs[-4:]
    front = 2 * (gp_ref.shape[1] // 3)
    rows = kept_ref.shape[2]
    grads = dot_first(n_ref[...], gp_ref[...])
    tail = dot_first(grad_ref[...], att_ref[...])[:, HEAD_DIM:]
    rest_ref[...] = jnp.concatenate([grads[:, front:], tail], axis=1).astype(LOW)
    all_ref[...] = grads[:, :front].astype(LOW).reshape(all_ref.shape)
    flag = flag_ref[0]
    for block in range(kept_ref.shape[1]):
        kept_ref[0, block] = all_ref[2 * block + flag]
        sent_ref[0, block] = all_ref[2 * block + 1 - flag]


def attention_grads(number, flag, normed, grad, gp, att, before=()):
    d, size = normed.shape[1], lax.axis_size("dp")
    width = gp.shape[1] // 3
    shape = jax.ShapeDtypeStruct
    pair = shape((2, size // 2, d // size, 2 * width), LOW)
    pair_spec = pl.BlockSpec((1,) + pair.shape[1:], lambda i: (number, 0, 0, 0))
    whole = lambda a: pl.BlockSpec(a.shape, lambda i: (0, 0), pipeline_mode=pl.Buffered(1))
    return pl.pallas_call(
        partial(attention_grads_kernel, number),
        grid=(1,),
        in_specs=[pl.BlockSpec(memory_space=pltpu.SMEM)]
        + [whole(a) for a in (normed, grad, gp, att)]
        + [pl.BlockSpec(memory_space=pl.ANY)] * len(before),
        out_specs=[pair_spec, pair_spec, pl.BlockSpec((d, 2 * width), lambda i: (0, 0))],
        out_shape=[pair, pair, shape((d, 2 * width), LOW)],
        scratch_shapes=[pltpu.VMEM((size, d // size, 2 * width), LOW)],
        input_output_aliases={5: 0, 6: 1} if before else {},
        compiler_params=params(16),
        cost_estimate=cost(4),
        name="attention_grads",
    )(flag, normed, grad, gp, att, *before)


def together(*values):
    return lax.optimization_barrier(values)


def swap(value, axis, bits):
    size = lax.axis_size(axis)
    return lax.ppermute(value, axis, [(i, i ^ bits) for i in range(size)])


def has(axis, bit):
    return (lax.axis_index(axis) // bit) % 2 == 1


def cat(a, b):
    return jnp.concatenate([a, b], axis=1)


def in_order(flag, own, other, axis):
    return jnp.concatenate([jnp.where(flag, other, own), jnp.where(flag, own, other)], axis=axis)


def far_bits():
    bit, bits = lax.axis_size("dp") // 2, []
    while bit > 1:
        bits.append(bit)
        bit //= 2
    return bits


def far_groups():
    at, groups = 2, []
    while at < lax.axis_size("dp"):
        size = min(4, lax.axis_size("dp") // at)
        groups.append((at, size))
        at *= size
    return groups


def far_place(group):
    at, size = group
    return (lax.axis_index("dp") // at) % size


def far_swaps(value, group):
    at, size = group
    return [swap(value, "dp", at * m) for m in range(1, size)]


def far_order(held, there, group):
    place, blocks = far_place(group), [held] + list(there)
    pick = lambda b: lax.select_n(place, *[blocks[b ^ p] for p in range(group[1])])
    return jnp.stack([pick(b) for b in range(group[1])])


def rows_of(held, there):
    return in_order(has("dp", 1), held[:, None], there[:, None], 1).reshape(-1, held.shape[-1])


def parted(grad):
    size = lax.axis_size("dp")
    parts = grad.reshape(size // 2, 2, grad.shape[0] // size, grad.shape[1])
    flag = has("dp", 1)
    return jnp.where(flag, parts[:, 1], parts[:, 0]), jnp.where(flag, parts[:, 0], parts[:, 1])


def added(a, b):
    return (a.astype(WIDE) + b.astype(WIDE)).astype(LOW)


class Gather:
    def __init__(self, piece, parts, direct):
        self.held, self.parts, self.direct = piece[None], parts, direct
        self.steps = far_groups() if direct else far_bits()
        while len(self.steps) > (1 if direct else 2):
            self.far_start()
            self.far_end(self.there)

    def far_start(self):
        if self.direct:
            self.there = far_swaps(self.held, self.steps[0])
        else:
            self.there = swap(self.held, "dp", self.steps[0])

    def far_end(self, there):
        step = self.steps.pop(0)
        if self.direct:
            held = far_order(self.held, there, step)
        else:
            held = in_order(has("dp", step), self.held[:, None], there[:, None], 1)
        self.held = held.reshape((-1,) + held.shape[2:])

    def near_start(self):
        n = self.held.shape[-1] // (2 * self.parts)
        blocks = [self.held[..., i * n : (i + 1) * n] for i in range(2 * self.parts)]
        self.a, self.b = jnp.stack(blocks[: self.parts]), jnp.stack(blocks[self.parts :])
        self.there = swap(self.a, "dp", 1), swap(self.b, "tensor", 2)

    def near_end(self, there):
        self.a = [rows_of(a, x) for a, x in zip(self.a, there[0])]
        self.b = [jnp.stack([b, y]) for b, y in zip(self.b, there[1])]

    def last_start(self, part):
        self.there = swap(self.a[part], "tensor", 2), swap(self.b[part], "dp", 1)

    def last_end(self, part, there):
        return self.a[part], there[0], self.b[part], there[1]


class Scatter:
    def __init__(self):
        self.parts, self.extra = [], None

    def start(self, kept, sent, b_own, b_other):
        self.there = swap(sent, "dp", 1), swap(b_other, "tensor", 2)
        self.parts.append((kept, b_own))

    def near_end(self, part, there):
        kept, b_own = self.parts[part]
        b, b_sent = parted(added(b_own, there[1]))
        self.parts[part] = added(kept[0], there[0][0]), b, added(kept[1], there[0][1]), b_sent

    def last_start(self):
        self.a, self.b, sent_a, sent_b = (jnp.stack(v) for v in zip(*self.parts))
        self.sent = sent_a, sent_b
        self.there = swap(sent_a, "tensor", 2), swap(sent_b, "dp", 1)

    def last_end(self, there):
        a, b = added(self.a, there[0]), added(self.b, there[1])
        self.held = jnp.concatenate(list(a) + list(b), axis=2)
        self.groups = far_groups()
        self.far_start()

    def far_start(self):
        at, size = self.groups[0]
        parts = self.held.reshape((-1, size) + self.held.shape[1:])
        place = far_place(self.groups[0])
        pick = lambda m: lax.dynamic_index_in_dim(parts, place ^ m, 1, keepdims=False)
        self.held = pick(0)
        if self.extra is None:
            self.there = [swap(pick(m), "dp", at * m) for m in range(1, size)]
        else:
            high = lax.reduce_precision(self.extra, 8, 7)
            extra = [v.astype(LOW) for v in (high, self.extra - high)]
            n = self.held.shape[-1]
            self.there = [
                swap(jnp.concatenate([pick(m).reshape(-1, n)] + extra), "dp", at * m) for m in range(1, size)
            ]

    def far_end(self, there):
        total = self.held.astype(WIDE)
        rows = total.shape[0] * total.shape[1]
        for part in there:
            if self.extra is not None:
                high, low = jnp.split(part[rows:].astype(WIDE), 2)
                self.extra = self.extra + (high + low)
                part = part[:rows].reshape(total.shape)
            total = total + part.astype(WIDE)
        self.groups.pop(0)
        if not self.groups:
            return total[0]
        self.held = total.astype(LOW)
        self.far_start()
        return self.far_end(self.there)


def body(
    hidden, segment_ids, norm1_gain, norm1_bias, w_qkv, qv_bias, w_out, out_bias,
    norm2_gain, norm2_bias, w_up, up_bias, w_down, down_bias, cotangent,
):
    mine, d = hidden.shape
    width, units = w_qkv.shape[2], w_up.shape[1]
    half = units // 2
    core = has("tensor", 1)
    row = lambda v: v.reshape(1, -1)
    low_dot = lambda a, b: dot_first(a, b).astype(LOW)

    flag = has("dp", 1).astype(jnp.int32).reshape(1)

    g0 = Gather(jnp.concatenate([w_qkv[0], w_qkv[1], w_qkv[2], w_out.T], axis=1), 1, True)
    g0.far_start()
    units_piece = cat(w_up, w_down.T)

    pair = jnp.concatenate([hidden, cotangent], axis=1)
    both = in_order(core, pair, swap(pair, "tensor", 1), 0)
    seg = lax.dynamic_index_in_dim(segment_ids, lax.axis_index("tensor") // 2, 0, keepdims=False)
    seg = seg.reshape(-1, 1)
    here = lax.axis_index("tensor") % 2 * mine
    there = mine - here
    biases = jnp.concatenate([qv_bias.reshape(-1), up_bias])
    other_biases = swap(biases, "tensor", 2)
    none = jnp.zeros((width,), WIDE)
    shift = jnp.stack(
        [jnp.concatenate([v[:width], none, v[width : 2 * width]]) for v in (biases, other_biases)]
    )
    scale = jnp.concatenate([none + HEAD_DIM ** (-0.5), none + 1.0, none + 1.0]).reshape(1, -1)

    swaps, units_piece = together(g0.there, units_piece)
    g0.far_end(swaps)
    g0.near_start()
    g1 = Gather(units_piece, 2, False)
    g1.far_start()
    swaps, swaps1 = together(g0.there, g1.there)
    g0.near_end(swaps)
    g0.last_start(0)
    g1.far_end(swaps1)
    g1.far_start()
    swaps, swaps1 = together(g0.there, g1.there)
    g1.far_end(swaps1)
    g1.near_start()
    n1, p0, p1, w0, w1 = project(
        flag, both, row(norm1_gain), row(norm1_bias), *g0.last_end(0, swaps), shift, scale
    )
    att1, log1 = attend(p1, seg)
    swaps, log1 = together(g1.there, log1)
    g1.near_end(swaps)
    g1.last_start(0)
    att0, log0 = attend(p0, seg, (log1, g1.a[0], g1.b[0]))
    unit_bias = lambda at: row(jnp.concatenate([up_bias[at : at + half], other_biases[2 * width + at :][:half]]))
    swaps, log0, att0 = together(g1.there, log0, att0)
    cut = w0.shape[1] - att0.shape[1]
    pa = (dot_last(att0, w0[:, cut:]) + dot_last(att1, w1[:, cut:])).astype(LOW)
    pb = swap(pa, "tensor", 1)
    first_units = g1.last_end(0, swaps)
    g1.last_start(1)
    mlp, ga, units1, *grads, middle, n2 = mlp_pass(
        True, flag, both, both, (pa, pb, row(out_bias), row(norm2_gain), row(norm2_bias)),
        unit_bias(0), *first_units,
    )
    swaps, units1 = together(g1.there, units1)
    s1 = Scatter()
    s1.start(*grads)
    mlp, ga, units2, *grads = mlp_pass(
        False, flag, n2, both, (mlp, ga), unit_bias(half), *g1.last_end(1, swaps), (units1,)
    )
    kept, sent, own, other = grads
    swaps, units2, ga, sent, other = together(s1.there, units2, ga, sent, other)
    gb = swap(ga, "tensor", 1)
    s1.start(kept, sent, own, other)
    grad_mid, grad_attn, gatt0, gatt1, sums = norm_back(
        middle, both, ga, gb, row(norm2_gain), w0, w1, att0.shape[1], (units2,)
    )
    swaps, sums = together(swaps, sums)
    s1.near_end(0, swaps)
    gp1, gsum1 = attend_back(p1, seg, att1, log1, gatt1)
    swaps, gsum1 = together(s1.there, gsum1)
    s1.near_end(1, swaps)
    s1.last_start()
    kept, sent, last1 = attention_grads(1, flag, n1, grad_attn, gp1, att1)
    gp0, gsum0 = attend_back(p0, seg, att0, log0, gatt0, s1.sent + (gsum1,))
    kept, sent, last0 = attention_grads(0, flag, n1, grad_attn, gp0, att0, (kept, sent))
    swaps, gsum0, here, own_hidden, units1, units2 = together(s1.there, gsum0, here, hidden, units1, units2)
    there = mine - here
    s0 = Scatter()
    s0.start(kept, sent, last0, last1)
    s1.last_end(swaps)

    def branch(start):
        cut_rows = lambda v: lax.dynamic_slice_in_dim(v, start, mine, 0)
        return dot_last(cut_rows(gp0), w0[:, : 3 * width]) + dot_last(cut_rows(gp1), w1[:, : 3 * width])

    from_there = swap(branch(there).astype(LOW), "tensor", 1)
    grad_normed1 = branch(here) + from_there.astype(WIDE)

    center, inverse = centered(own_hidden.astype(WIDE))
    normal = center * inverse
    f = grad_normed1 * norm1_gain
    grad_input = inverse * (f - jnp.mean(f, -1, keepdims=True) - normal * jnp.mean(f * normal, -1, keepdims=True))
    grad_hidden = (lax.dynamic_slice_in_dim(grad_mid, here, mine, 0) + grad_input).astype(LOW)
    norm1_sums = jnp.stack([jnp.sum(grad_normed1 * normal, 0), jnp.sum(grad_normed1, 0)])
    norm1_sums = norm1_sums + swap(norm1_sums, "tensor", 1)
    shared = jnp.concatenate([norm1_sums.reshape(-1), sums[:4].reshape(-1)])
    part = lambda gsum, at: jnp.concatenate(
        [gsum[0, :width], gsum[0, 2 * width :], units1[0, at : at + half], units2[0, at : at + half]]
    )

    mlp_there = swap(lax.dynamic_slice_in_dim(mlp, there, mine, 0), "tensor", 1)
    mlp_here = lax.dynamic_slice_in_dim(mlp, here, mine, 0)
    output = lax.dynamic_slice_in_dim(middle, here, mine, 0) + down_bias
    output = (output + (mlp_here.astype(WIDE) + mlp_there.astype(WIDE))).astype(LOW)

    (swaps,) = together(s0.there)
    own, other = part(gsum0, 0), part(gsum1, half)
    s0.near_end(0, swaps)
    s0.last_start()
    sent, output = together(jnp.concatenate([shared, own, other]), output)
    over_x = swap(sent, "dp", 1)
    over_y, over_both = swap(sent, "tensor", 2), lax.ppermute(
        sent, ("dp", "tensor"),
        [
            (i * lax.axis_size("tensor") + t, (i ^ 1) * lax.axis_size("tensor") + (t ^ 2))
            for i in range(lax.axis_size("dp"))
            for t in range(lax.axis_size("tensor"))
        ],
    )
    swaps, swaps1, over_x, over_y, over_both = together(s0.there, s1.there, over_x, over_y, over_both)
    full, units_here = 6 * d, 2 * width + units
    total = (sent + over_x)[: full + units_here]
    flipped = over_y + over_both
    total = total + jnp.concatenate([flipped[:full], flipped[full + units_here :]])
    s0.extra = jnp.pad(total, (0, -total.shape[0] % (8 * d))).reshape(-1, d)
    s0.last_end(swaps)
    grad1 = s1.far_end(swaps1)
    (swaps,) = together(s0.there)
    grad0 = s0.far_end(swaps)
    total = s0.extra.reshape(-1)[: total.shape[0]]
    norm1_gain_grad, norm1_bias_grad, gain2, bias2, out_grad, down_grad = (
        total[i * d : (i + 1) * d] for i in range(6)
    )
    own = total[full:]
    columns = lambda i: grad0[:, i * width : (i + 1) * width]
    return (
        output,
        grad_hidden,
        norm1_gain_grad,
        norm1_bias_grad,
        jnp.stack([columns(0), columns(1), columns(2)]),
        own[: 2 * width].reshape(2, width),
        columns(3).T,
        out_grad,
        gain2,
        bias2,
        grad1[:, :units],
        own[2 * width :],
        grad1[:, units:].T,
        down_grad,
    )


def solution(mesh):
    placed = (
        P(("dp", "tensor"), None),
        P("dp", None),
        P(),
        P(),
        P(None, "dp", "tensor"),
        P(None, "tensor"),
        P("tensor", "dp"),
        P(),
        P(),
        P(),
        P("dp", "tensor"),
        P("tensor"),
        P("tensor", "dp"),
        P(),
        P(("dp", "tensor"), None),
    )
    return jax.shard_map(
        body,
        mesh=mesh,
        in_specs=placed,
        out_specs=(
            P(("dp", "tensor"), None),
            P(("dp", "tensor"), None),
            P(),
            P(),
            P(None, "dp", "tensor"),
            P(None, "tensor"),
            P("tensor", "dp"),
            P(),
            P(),
            P(),
            P("dp", "tensor"),
            P("tensor"),
            P("tensor", "dp"),
            P(),
        ),
        check_vma=False,
    )
```
